32 devices in a mesh: tile: 2 (over y), date: 4 (over x, core), row: 4 (over z).
Axes of the slice: x: 2, y: 2, z: 4, core: 2. Of those that a mesh axis runs over, the one named last changes fastest.
Arguments:
- intensity: bfloat16 [64, 2, 512, 512], P('date', None, ('tile', 'row')), parts along dimension 2, may hold values from 0.019897461 to 1
- valid_mask: int32 [64, 8, 16, 2048], P(None, 'tile', ('date', 'row')), parts along dimension 1, may hold values 0 or 1
- day_index: int32 [64], replicated, may hold values from 0 to 364
Outputs:
- state_field: float32 [6, 8, 16, 2048], P(None, 'tile', ('date', 'row')), parts along dimension 1
The draws below stay inside these ranges and needn't reach their ends.
There are 2 independent parts, one for each index of `tile`. The reference program is written for one: setup_inputs(seed, part) draws one part's arguments, and reference() takes and returns one part's arrays. A program takes and returns all parts, laid end to end along the dimension named above; an argument that names none is the same for every part. Nothing has to cross between parts.
All inputs are finite; a program needn't handle non-finite values. No bound on the sum of `valid_mask` on one device may be relied on, other than what follows from the above.
Results may differ from the reference program's by a relative error of at most 0.0009.
Values may be sent and summed in bfloat16 or wider, within the bound.
No kernel may reach another device: no remote copies, remote signals or barrier semaphores. Data moves between devices by JAX's collectives and lax.ppermute only.
A program may use at most 64 MiB of HBM per device.

```python
import math
import jax
import jax.numpy as jnp
from jax import lax

DATES = 64
COLS = 512
RADIUS = 3
STATES = 6
ROWS = 256
SEG = 2048
N_DATE = 4
N_ROW = 4


def plant(entries, key, smallest, high):
    longest = entries.shape.index(max(entries.shape))
    spots = []
    for shift in (0, 1):
        where = [jax.random.randint(jax.random.fold_in(key, axis), (), 0, length) for axis, length in enumerate(entries.shape)]
        where[longest] = (where[longest] + shift) % entries.shape[longest]
        spots.append(tuple(where))
    return entries.at[spots[0]].set(smallest).at[spots[1]].set(high)


def steps_of(key, dims, shards, least, largest):
    loudness = 1.0
    for dim, shards_of in shards:
        heights = jax.random.uniform(jax.random.fold_in(jax.random.fold_in(key, 6), dim), (shards_of,), jnp.float32, least / len(shards), largest / len(shards))
        loudness = loudness * jnp.repeat(jnp.exp(heights), dims[dim] // shards_of).reshape((-1,) + (1,) * (len(dims) - 1 - dim))
    return loudness


def setup_inputs(seed: int = 0, part: int = 0) -> dict:
    key_list = jax.random.split(jax.random.key(seed), 4)
    part_keys = jax.random.split(jax.random.fold_in(key_list[3], part), 4)
    return {
        "intensity": jnp.clip(jnp.exp(math.log(1.0) - 3.9171631 * jax.random.uniform(part_keys[0], (DATES, 2, ROWS, COLS), jnp.float32) ** steps_of(part_keys[0], (DATES, 2, ROWS, COLS), ((0, 4), (2, 4)), -0.2, 0.2)), 0.019897461, 1.0).astype(jnp.bfloat16),
        "valid_mask": plant((jax.random.randint(part_keys[1], (DATES, N_ROW, N_DATE * N_ROW, SEG), 0, 4) < 3).astype(jnp.int32), jax.random.fold_in(part_keys[1], 1), 0, 1),
        "day_index": plant(jax.random.randint(key_list[2], (DATES,), 0, 365), jax.random.fold_in(key_list[2], 1), 0, 364).astype(jnp.int32),
    }


obs_noise = 0.05

def edge_count(positions, length):
    lower = jnp.maximum(positions - RADIUS, 0)
    upper = jnp.minimum(positions + RADIUS, length - 1)
    return (upper - lower + 1).astype(jnp.float32)

def box_images(images):
    field = images.astype(jnp.float32)
    height = field.shape[1]
    width = field.shape[2]
    padded_cols = jnp.pad(field, ((0, 0), (0, 0), (RADIUS, RADIUS)))
    col_sum = sum([padded_cols[:, :, k:k + width] for k in range(2 * RADIUS + 1)])
    padded_rows = jnp.pad(col_sum, ((0, 0), (RADIUS, RADIUS), (0, 0)))
    window = sum([padded_rows[:, k:k + height] for k in range(2 * RADIUS + 1)])
    row_count = edge_count(lax.iota(jnp.int32, height), height)
    col_count = edge_count(lax.iota(jnp.int32, width), width)
    return window / (row_count[:, None] * col_count[None, :])

def harmonic_fit(vv_series, vh_series, keep_flags, day_vector):
    phase_angle = day_vector.astype(jnp.float32) * (2.0 * math.pi / 365.0)
    ones_row = jnp.ones_like(phase_angle)
    zero_row = jnp.zeros_like(phase_angle)
    base_rows = [ones_row, jnp.cos(phase_angle), jnp.sin(phase_angle), jnp.cos(2.0 * phase_angle), jnp.sin(2.0 * phase_angle)]
    design_vv = jnp.stack(base_rows + [zero_row])
    design_vh = jnp.stack(base_rows + [ones_row])
    pair_list = [(a, b) for a in range(STATES) for b in range(a, STATES)]
    pair_table = jnp.stack([design_vv[a] * design_vv[b] + design_vh[a] * design_vh[b] for a, b in pair_list])
    highest = lax.Precision.HIGHEST
    pair_sums = jnp.dot(pair_table, keep_flags, precision=highest, preferred_element_type=jnp.float32) / obs_noise
    vv_obs = jnp.log(vv_series.astype(jnp.float32)) * keep_flags
    vh_obs = jnp.log(vh_series.astype(jnp.float32)) * keep_flags
    right = jnp.dot(design_vv, vv_obs, precision=highest, preferred_element_type=jnp.float32)
    right = (right + jnp.dot(design_vh, vh_obs, precision=highest, preferred_element_type=jnp.float32)) / obs_noise
    normal = {}
    for index, (a, b) in enumerate(pair_list):
        entry = pair_sums[index]
        if a == b:
            entry = entry + 1.0
        normal[b, a] = entry
    lower = {}
    for i in range(STATES):
        for j in range(i + 1):
            total = normal[i, j]
            for k in range(j):
                total = total - lower[i, k] * lower[j, k]
            if i == j:
                lower[i, i] = jnp.sqrt(total)
            else:
                lower[i, j] = total / lower[j, j]
    middle = []
    for i in range(STATES):
        total = right[i]
        for k in range(i):
            total = total - lower[i, k] * middle[k]
        middle.append(total / lower[i, i])
    solved = [None] * STATES
    for i in reversed(range(STATES)):
        total = middle[i]
        for k in range(i + 1, STATES):
            total = total - lower[k, i] * solved[k]
        solved[i] = total / lower[i, i]
    return jnp.stack(solved)

def reference(intensity, valid_mask, day_index):

    def accumulate(running, images):
        return (running + images.astype(jnp.float32) / box_images(images), None)
    start = jnp.zeros((2, ROWS, COLS), jnp.float32)
    ratio_sum, unused = lax.scan(accumulate, start, intensity)

    def filter_date(images):
        return (box_images(images) * (ratio_sum / DATES)).astype(jnp.bfloat16)
    filtered = lax.map(filter_date, intensity)
    keep_flags = valid_mask.reshape(DATES, ROWS * COLS).astype(jnp.float32)
    vv_series = filtered[:, 0].reshape(DATES, ROWS * COLS)
    vh_series = filtered[:, 1].reshape(DATES, ROWS * COLS)
    state_grid = harmonic_fit(vv_series, vh_series, keep_flags, day_index)
    return state_grid.reshape(STATES, N_ROW, N_DATE * N_ROW, SEG)
```

```python
import functools
import math

import jax
import jax.numpy as jnp
from jax import lax
from jax.experimental import pallas as pl
from jax.experimental.pallas import tpu as pltpu
from jax.sharding import PartitionSpec as P

RADIUS = 3
STATES = 6
HALO = 4
LANES = 128
HARMONICS = 9
NOISE = 0.05
CODE_STEPS = 8192.0
VMEM_BYTES = 40 * 1024 * 1024

f32 = jnp.float32
PAIRS = [(i, j) for i in range(STATES) for j in range(i)]


def partners(count, k):
    return [(i, i ^ k) for i in range(count)]


def edge_count(positions, length):
    lower = jnp.maximum(positions - RADIUS, 0)
    upper = jnp.minimum(positions + RADIUS, length - 1)
    return (upper - lower + 1).astype(f32)


def whole():
    return pl.BlockSpec(memory_space=pltpu.VMEM)


def scalars():
    return pl.BlockSpec(memory_space=pltpu.SMEM)


def params():
    return pltpu.CompilerParams(vmem_limit_bytes=VMEM_BYTES)


def flags_kernel(mask_ref, *out_refs):
    r = lax.axis_index("row")
    for k, out_ref in enumerate(out_refs):
        out_ref[...] = mask_ref[:, r ^ k].astype(f32).astype(jnp.bfloat16)


def cast_flags(mask, pieces):
    dates, blocks, chunks, lanes = mask.shape
    step = 16 if dates % 16 == 0 else dates
    return pl.pallas_call(
        flags_kernel,
        grid=(dates // step,),
        in_specs=[pl.BlockSpec((step, blocks, chunks, lanes), lambda t: (t, 0, 0, 0))],
        out_specs=[pl.BlockSpec((step, chunks, lanes), lambda t: (t, 0, 0))] * pieces,
        out_shape=[jax.ShapeDtypeStruct((dates, chunks, lanes), jnp.bfloat16)] * pieces,
        compiler_params=params(),
        name="cast_flags",
    )(mask)


def box_kernel(
    ks, x_ref, top_ref, bottom_ref, *refs
):
    code_refs = refs[: len(ks)]
    ratio_refs = refs[len(ks) : 2 * len(ks)]
    band, edges, scale, sums = refs[2 * len(ks) :]
    step = pl.program_id(0)
    d = lax.axis_index("date")
    r = lax.axis_index("row")
    dates, pols, rows, cols = x_ref.shape
    quarter = code_refs[0].shape[2]
    tiles = cols // LANES
    half = (d ^ ks[0]) // 2
    span = rows // 2 + 16
    first = pl.multiple_of(half * (rows // 2 - 16), 16)

    @pl.when(step == 0)
    def _():
        near = (
            jnp.abs(
                lax.broadcasted_iota(jnp.int32, (cols, cols), 0)
                - lax.broadcasted_iota(jnp.int32, (cols, cols), 1)
            )
            <= RADIUS
        )
        band[...] = near.astype(f32).astype(jnp.bfloat16)
        for side, ref in enumerate((top_ref, bottom_ref)):
            edge = jnp.dot(ref[...], band[...], preferred_element_type=f32)
            for c in range(tiles):
                edges[side, c] = edge[:, c * LANES : (c + 1) * LANES]
        height = rows * lax.axis_size("row")
        col = edge_count(lax.broadcasted_iota(jnp.int32, (quarter, cols), 1), cols)
        for n, k in enumerate(ks):
            row = edge_count(
                r * rows
                + quarter * (d ^ k)
                + lax.broadcasted_iota(jnp.int32, (quarter, cols), 0),
                height,
            )
            scale[n] = 1.0 / (row * col)
            ratio_refs[n][...] = jnp.zeros_like(ratio_refs[n])

    images = dates * pols
    x = x_ref[:, :, pl.ds(first, span), :].reshape(images * span, cols)
    summed = jnp.dot(x, band[...], preferred_element_type=f32)
    for i in range(images):
        at = (step * images + i) * HALO
        for c in range(tiles):
            lanes = slice(c * LANES, (c + 1) * LANES)
            sums[i, c, 8 : 8 + span] = summed[i * span : (i + 1) * span, lanes]
            sums[i, c, 8 - HALO : 8] = edges[0, c, pl.ds(at, HALO)]
            sums[i, c, 8 + span : 8 + span + HALO] = edges[1, c, pl.ds(at, HALO)]
    for n, k in enumerate(ks):
        q = d ^ k
        base = 8 + half * 16 + quarter * (q % 2)
        for pol in range(pols):
            for c in range(tiles):
                lanes = slice(c * LANES, (c + 1) * LANES)
                total = ratio_refs[n][pol, :, lanes]
                for t in range(dates):
                    i = t * pols + pol
                    window = sums[i, c, pl.ds(base - RADIUS, quarter)]
                    for shift in range(1 - RADIUS, RADIUS + 1):
                        window = window + sums[i, c, pl.ds(base + shift, quarter)]
                    mean = window * scale[n, :, lanes]
                    cells = x_ref[t, pol, pl.ds(pl.multiple_of(quarter * q, 16), quarter), lanes]
                    total = total + cells.astype(f32) / mean
                    code = jnp.log(mean) * CODE_STEPS - 0.5
                    code_refs[n][t, pol, :, lanes] = code.astype(jnp.int32).astype(jnp.int16)
                ratio_refs[n][pol, :, lanes] = total


def box_codes(intensity, top, bottom, ks, quarter):
    dates, pols, rows, cols = intensity.shape
    step = 2 if dates % 2 == 0 else 1
    images = step * pols
    tiles = cols // LANES
    count = len(ks)
    return pl.pallas_call(
        functools.partial(box_kernel, ks),
        grid=(dates // step,),
        in_specs=[
            pl.BlockSpec((step, pols, rows, cols), lambda t: (t, 0, 0, 0)),
            pl.BlockSpec(top.shape, lambda t: (0, 0)),
            pl.BlockSpec(bottom.shape, lambda t: (0, 0)),
        ],
        out_specs=[pl.BlockSpec((step, pols, quarter, cols), lambda t: (t, 0, 0, 0))] * count
        + [pl.BlockSpec((pols, quarter, cols), lambda t: (0, 0, 0))] * count,
        out_shape=[jax.ShapeDtypeStruct((dates, pols, quarter, cols), jnp.int16)] * count
        + [jax.ShapeDtypeStruct((pols, quarter, cols), f32)] * count,
        scratch_shapes=[
            pltpu.VMEM((cols, cols), jnp.bfloat16),
            pltpu.VMEM((2, tiles, dates * pols * HALO, LANES), f32),
            pltpu.VMEM((count, quarter, cols), f32),
            pltpu.VMEM((images, tiles, rows // 2 + 32, LANES), f32),
        ],
        compiler_params=params(),
        name="box_codes",
    )(intensity, top, bottom)


def factor_kernel(chunked, table_ref, *refs):
    piece_refs = refs[:-3]
    flags_ref, factor_ref, lines = refs[-3:]
    r = lax.axis_index("row")
    dates, quarter, cols = flags_ref.shape
    tiles = cols // LANES
    for k, piece_ref in enumerate(piece_refs):
        chunks = piece_ref.shape[1]
        at = pl.multiple_of((r ^ k) * chunks, 16) if chunked else 0
        lines[:, pl.ds(at, chunks)] = piece_ref[...].astype(f32)
    for h in range(quarter // 8):
        down = slice(h * 8, (h + 1) * 8)

        def add_date(t, totals):
            new = []
            for c in range(tiles):
                flag = lines[t, pl.ds(h * 8 * tiles + c, 8, stride=tiles)]
                flags_ref[t, down, c * LANES : (c + 1) * LANES] = flag
                new.append(totals[c * HARMONICS] + flag)
                for n in range(1, HARMONICS):
                    new.append(totals[c * HARMONICS + n] + flag * table_ref[n, t])
            return tuple(new)

        zero = jnp.zeros((8, LANES), f32)
        totals = lax.fori_loop(0, dates, add_date, (zero,) * (tiles * HARMONICS), unroll=4)
        for c in range(tiles):
            lanes = slice(c * LANES, (c + 1) * LANES)
            m0, c1, s1, c2, s2, c3, s3, c4, s4 = totals[c * HARMONICS : (c + 1) * HARMONICS]
            normal = {
                (0, 0): 2.0 * m0 + NOISE,
                (1, 0): 2.0 * c1,
                (2, 0): 2.0 * s1,
                (3, 0): 2.0 * c2,
                (4, 0): 2.0 * s2,
                (1, 1): m0 + c2 + NOISE,
                (2, 1): s2,
                (3, 1): c1 + c3,
                (4, 1): s1 + s3,
                (2, 2): m0 - c2 + NOISE,
                (3, 2): s3 - s1,
                (4, 2): c1 - c3,
                (3, 3): m0 + c4 + NOISE,
                (4, 3): s4,
                (4, 4): m0 - c4 + NOISE,
                (5, 0): m0,
                (5, 1): c1,
                (5, 2): s1,
                (5, 3): c2,
                (5, 4): s2,
                (5, 5): m0 + NOISE,
            }
            lower = {}
            inverse = {}
            for i in range(STATES):
                for j in range(i + 1):
                    total = normal[i, j]
                    for k in range(j):
                        total = total - lower[i, k] * lower[j, k]
                    if i == j:
                        inverse[i] = 1.0 / jnp.sqrt(total)
                    else:
                        lower[i, j] = total * inverse[j]
            planes = [lower[p] for p in PAIRS] + [inverse[i] for i in range(STATES)]
            planes += [m0, c1, s1, c2, s2]
            for n, plane in enumerate(planes):
                factor_ref[n, down, lanes] = plane


PLANES = len(PAIRS) + STATES + STATES - 1


def factor(table, pieces, quarter, cols):
    dates = pieces[0].shape[0]
    return pl.pallas_call(
        functools.partial(factor_kernel, len(pieces) > 1),
        in_specs=[scalars()] + [whole()] * len(pieces),
        out_specs=[whole()] * 2,
        out_shape=[
            jax.ShapeDtypeStruct((dates, quarter, cols), f32),
            jax.ShapeDtypeStruct((PLANES, quarter, cols), f32),
        ],
        scratch_shapes=[pltpu.VMEM((dates, quarter * cols // LANES, LANES), f32)],
        compiler_params=params(),
        name="factor",
    )(table, *pieces)


def right_sums(ks, table_ref, flags_ref, code_refs, lanes):
    d = lax.axis_index("date")
    quarter = flags_ref.shape[1]
    sums = [jnp.zeros((quarter, LANES), f32) for _ in range(STATES)]
    for k, code_ref in zip(ks, code_refs):
        dates = code_ref.shape[0]
        for t in range(dates):
            at = (d ^ k) * dates + t
            flag = flags_ref[at, :, lanes]
            vv = code_ref[t, 0, :, lanes].astype(jnp.int32).astype(f32)
            vh = code_ref[t, 1, :, lanes].astype(jnp.int32).astype(f32) * flag
            both = vv * flag + vh
            sums[0] = sums[0] + both
            for n in range(1, STATES - 1):
                sums[n] = sums[n] + both * table_ref[n, at]
            sums[STATES - 1] = sums[STATES - 1] + vh
    return sums


def right_kernel(ks, table_ref, flags_ref, *refs):
    code_refs, out_ref = refs[:-1], refs[-1]
    for c in range(flags_ref.shape[2] // LANES):
        lanes = slice(c * LANES, (c + 1) * LANES)
        for n, total in enumerate(right_sums(ks, table_ref, flags_ref, code_refs, lanes)):
            out_ref[n, :, lanes] = total


def right_part(table, flags, codes, ks):
    dates, quarter, cols = flags.shape
    return pl.pallas_call(
        functools.partial(right_kernel, ks),
        in_specs=[scalars()] + [whole()] * (1 + len(codes)),
        out_specs=whole(),
        out_shape=jax.ShapeDtypeStruct((STATES, quarter, cols), f32),
        compiler_params=params(),
        name="right_part",
    )(table, flags, *codes)


def solve_kernel(ks, ratios, pieces, table_ref, flags_ref, factor_ref, part_ref, *refs):
    code_refs = refs[: len(ks)]
    ratio_refs = refs[len(ks) : len(ks) + ratios]
    out_refs = refs[len(ks) + ratios : -1]
    lines = refs[-1]
    r = lax.axis_index("row")
    dates, quarter, cols = flags_ref.shape
    tiles = cols // LANES
    for c in range(tiles):
        lanes = slice(c * LANES, (c + 1) * LANES)
        sums = right_sums(ks, table_ref, flags_ref, code_refs, lanes)
        logs = []
        for pol in range(2):
            total = ratio_refs[0][pol, :, lanes]
            for ratio_ref in ratio_refs[1:]:
                total = total + ratio_ref[pol, :, lanes]
            logs.append(jnp.log(total * (1.0 / dates)))
        bases = [factor_ref[len(PAIRS) + STATES + n, :, lanes] for n in range(STATES - 1)]
        right = [
            (sums[n] + part_ref[n, :, lanes]) * (1.0 / CODE_STEPS) for n in range(STATES)
        ]
        both = logs[0] + logs[1]
        for n in range(STATES - 1):
            right[n] = right[n] + both * bases[n]
        right[STATES - 1] = right[STATES - 1] + logs[1] * bases[0]
        lower = {p: factor_ref[n, :, lanes] for n, p in enumerate(PAIRS)}
        inverse = [factor_ref[len(PAIRS) + n, :, lanes] for n in range(STATES)]
        middle = []
        for i in range(STATES):
            total = right[i]
            for k in range(i):
                total = total - lower[i, k] * middle[k]
            middle.append(total * inverse[i])
        solved = [None] * STATES
        for i in reversed(range(STATES)):
            total = middle[i]
            for k in range(i + 1, STATES):
                total = total - lower[k, i] * solved[k]
            solved[i] = total * inverse[i]
        for n in range(STATES):
            for h in range(quarter // 8):
                lines[n, pl.ds(h * 8 * tiles + c, 8, stride=tiles)] = solved[n][
                    h * 8 : (h + 1) * 8
                ]
    for k, out_ref in enumerate(out_refs):
        chunks = out_ref.shape[1]
        at = pl.multiple_of((r ^ k) * chunks, 8) if pieces > 1 else 0
        out_ref[...] = lines[:, pl.ds(at, chunks)]


def solve(table, flags, factors, part, codes, ratios, ks, pieces):
    dates, quarter, cols = flags.shape
    chunks = quarter * cols // LANES
    return pl.pallas_call(
        functools.partial(solve_kernel, ks, len(ratios), pieces),
        in_specs=[scalars()] + [whole()] * (3 + len(codes) + len(ratios)),
        out_specs=[whole()] * pieces,
        out_shape=[jax.ShapeDtypeStruct((STATES, chunks // pieces, LANES), f32)] * pieces,
        scratch_shapes=[pltpu.VMEM((STATES, chunks, LANES), f32)],
        compiler_params=params(),
        name="solve",
    )(table, flags, factors, part, *codes, *ratios)


def gather_kernel(*refs):
    r = lax.axis_index("row")
    for k, in_ref in enumerate(refs[:-1]):
        refs[-1][:, r ^ k] = in_ref[...]


def gather_states(parts):
    states, chunks, lanes = parts[0].shape
    return pl.pallas_call(
        gather_kernel,
        in_specs=[whole()] * len(parts),
        out_specs=whole(),
        out_shape=jax.ShapeDtypeStruct((states, len(parts), chunks, lanes), f32),
        compiler_params=params(),
        name="gather_states",
    )(*parts)


def harmonics(day_index):
    phase = day_index.astype(f32) * (2.0 * math.pi / 365.0)
    row = lax.broadcasted_iota(jnp.int32, (HARMONICS, day_index.shape[0]), 0)
    angle = ((row + 1) // 2).astype(f32) * phase[None, :]
    return jnp.where(row % 2 == 1, jnp.cos(angle), jnp.where(row == 0, 1.0, jnp.sin(angle)))


def body(intensity, valid_mask, day_index):
    rows, cols = intensity.shape[2:]
    date_devices = lax.axis_size("date")
    row_devices = lax.axis_size("row")
    quarter = rows // date_devices
    all_dates = valid_mask.shape[0]
    segment = quarter * cols // row_devices
    chunks = segment // LANES
    direct = row_devices in (2, 4) and chunks % 16 == 0

    edges = [
        cells.reshape(-1, cols)
        for cells in (intensity[:, :, rows - HALO :], intensity[:, :, :HALO])
    ]
    ring = range(row_devices - 1)
    top = lax.ppermute(edges[0], "row", [(i, i + 1) for i in ring])
    bottom = lax.ppermute(edges[1], "row", [(i + 1, i) for i in ring])

    if direct:
        lines = valid_mask.reshape(all_dates, row_devices, chunks, LANES)
        flags = cast_flags(lines, row_devices)
        flags = [flags[0]] + [
            lax.ppermute(flags[k], "row", partners(row_devices, k)) for k in range(1, row_devices)
        ]
    else:
        moved = lax.all_to_all(
            valid_mask.astype(jnp.bfloat16), "row", split_axis=1, concat_axis=2, tiled=True
        )
        flags = [moved.reshape(all_dates, row_devices * chunks, LANES)]

    table = harmonics(day_index)

    far = box_codes(intensity, top, bottom, (2, 3), quarter)
    moved_codes = {}
    moved_ratios = {}
    for n, k in enumerate((2, 3)):
        moved_ratios[k] = lax.ppermute(far[2 + n], "date", partners(date_devices, k))
        moved_codes[k] = lax.ppermute(far[n], "date", partners(date_devices, k))
    near = box_codes(intensity, top, bottom, (0, 1), quarter)
    moved_codes[0], moved_ratios[0] = near[0], near[2]
    moved_codes[1] = lax.ppermute(near[1], "date", partners(date_devices, 1))
    moved_ratios[1] = lax.ppermute(near[3], "date", partners(date_devices, 1))

    image_flags, factors = factor(table, flags, quarter, cols)
    part = right_part(table, image_flags, [moved_codes[0], moved_codes[1]], (0, 1))
    pieces = row_devices if direct else 1
    states = solve(
        table,
        image_flags,
        factors,
        part,
        [moved_codes[2], moved_codes[3]],
        [moved_ratios[k] for k in range(date_devices)],
        (2, 3),
        pieces,
    )
    if direct:
        states = [states[0]] + [
            lax.ppermute(states[k], "row", partners(row_devices, k)) for k in range(1, row_devices)
        ]
        return gather_states(states).reshape(STATES, row_devices, 1, segment)
    states = states[0].reshape(STATES, 1, row_devices, segment)
    return lax.all_to_all(states, "row", split_axis=2, concat_axis=1, tiled=True)


def solution(mesh):
    return jax.shard_map(
        body,
        mesh=mesh,
        in_specs=(
            P("date", None, ("tile", "row"), None),
            P(None, "tile", ("date", "row"), None),
            P(),
        ),
        out_specs=P(None, "tile", ("date", "row"), None),
        check_vma=False,
    )
```

```python
import functools
import math

import jax
import jax.numpy as jnp
import numpy as np
from jax import lax
from jax.experimental import pallas as pl
from jax.experimental.pallas import tpu as pltpu
from jax.sharding import PartitionSpec as P

RADIUS = 3
STATES = 6
HALO = 4
GROUP = 8
LANES = 128
HARMONICS = 9
NOISE = 0.05
CODE_STEPS = 8192.0
REST_STEPS = 32768.0
VMEM_BYTES = 16 * 1024 * 1024

SHORT = pl.CostEstimate(flops=1000, bytes_accessed=1000, transcendentals=0)

f32 = jnp.float32
i32 = jnp.int32
PAIRS = [(i, j) for i in range(STATES) for j in range(i)]
PLANES = len(PAIRS) + STATES


def partners(count, k):
    return [(i, i ^ k) for i in range(count)]


def ratio_steps(dates):
    return 2.0 ** math.floor(math.log2(32767 / ((2 * RADIUS + 1) ** 2 * dates)))


def edge_count(positions, length):
    lower = jnp.maximum(positions - RADIUS, 0)
    upper = jnp.minimum(positions + RADIUS, length - 1)
    return (upper - lower + 1).astype(f32)


def whole():
    return pl.BlockSpec(memory_space=pltpu.VMEM)


def anywhere():
    return pl.BlockSpec(memory_space=pl.ANY)


def scalars():
    return pl.BlockSpec(memory_space=pltpu.SMEM)


def params():
    return pltpu.CompilerParams(vmem_limit_bytes=VMEM_BYTES)


def tiles_of(width):
    return [slice(c, c + LANES) for c in range(0, width, LANES)]


def flags_kernel(pieces, mask_ref, *refs):
    r = lax.axis_index("row")
    for k, out_ref in enumerate(refs[-pieces:]):
        chunks = out_ref.shape[1]
        at = pl.multiple_of((r ^ k) * chunks, 16)
        out_ref[...] = mask_ref[:, pl.ds(at, chunks)].astype(f32).astype(jnp.bfloat16)


def cast_flags(lines, pieces, after=()):
    dates, count, lanes = lines.shape
    return pl.pallas_call(
        functools.partial(flags_kernel, pieces),
        in_specs=[whole()] + [anywhere()] * len(after),
        out_specs=[whole()] * pieces,
        out_shape=[pltpu.VMEM((dates, count // pieces, lanes), jnp.bfloat16)] * pieces,
        compiler_params=params(),
        cost_estimate=SHORT,
        name="cast_flags",
    )(lines, *after)


def box_kernel(ks, parts, x_ref, *refs):
    first_call = 1 not in parts
    if first_call:
        outs = refs[-7:-5]
        refs[-5][...] = jnp.zeros_like(refs[-5])
        band, sums, cells_ref, arrived = refs[-4:]
        batch = x_ref.shape[0] // arrived.shape[0]
        copies = [
            pltpu.make_async_copy(
                x_ref.at[pl.ds(n * batch, batch)],
                cells_ref.at[pl.ds(n * batch, batch)],
                arrived.at[n],
            )
            for n in range(arrived.shape[0])
        ]
        for copy in copies:
            copy.start()
        x_ref = cells_ref
    else:
        outs = refs[-6:-4]
        refs[-4][...] = jnp.zeros_like(refs[-4])
        band, sums, edges = refs[-3:]
        batch = 4
    d = lax.axis_index("date")
    r = lax.axis_index("row")
    dates, pols, rows, cols = x_ref.shape
    quarter = rows // lax.axis_size("date")
    half = (d ^ ks[0]) // 2
    span = rows // 2 + 16
    first = pl.multiple_of(half * (rows // 2 - 16), 16)
    images = dates * pols

    near = (
        jnp.abs(
            lax.broadcasted_iota(i32, (cols, cols), 0) - lax.broadcasted_iota(i32, (cols, cols), 1)
        )
        <= RADIUS
    )
    band[...] = near.astype(f32).astype(jnp.bfloat16)
    if 1 in parts:
        edges[...] = jnp.dot(refs[0][...], band[...], preferred_element_type=f32)
        place = jnp.where(half == 0, GROUP - HALO, GROUP + span)
        for i in range(images):
            for c, lanes in enumerate(tiles_of(cols)):
                sums[i, c, pl.ds(place, HALO)] = edges[i * HALO : (i + 1) * HALO, lanes]
    for t in range(0, dates, batch):
        if first_call:
            copies[t // batch].wait()
        x = x_ref[t : t + batch, :, pl.ds(first, span), :].reshape(batch * pols * span, cols)
        summed = jnp.dot(x, band[...], preferred_element_type=f32)
        for i in range(batch * pols):
            for c, lanes in enumerate(tiles_of(cols)):
                sums[t * pols + i, c, GROUP : GROUP + span] = summed[
                    i * span : (i + 1) * span, lanes
                ]

    height = rows * lax.axis_size("row")
    col = edge_count(lax.broadcasted_iota(i32, (GROUP, cols), 1), cols)
    steps = ratio_steps(dates)
    for n, k in enumerate(ks):
        q = d ^ k
        for p, part in enumerate(parts):
            group = half if part else 1 - half
            top = quarter * q + GROUP * group
            base = GROUP + top - first
            row = edge_count(r * rows + top + lax.broadcasted_iota(i32, (GROUP, cols), 0), height)
            scale = 1.0 / (row * col)
            out = outs[n].at[p] if len(parts) > 1 else outs[n]
            cells_at = pl.multiple_of(quarter * q, 16)

            def add_date(t, totals):
                new = []
                for c, lanes in enumerate(tiles_of(cols)):
                    codes = []
                    for pol in range(pols):
                        i = t * pols + pol
                        window = sums[i, c, pl.ds(base - RADIUS, GROUP)]
                        for shift in range(1 - RADIUS, RADIUS + 1):
                            window = window + sums[i, c, pl.ds(base + shift, GROUP)]
                        mean = window * scale[:, lanes]
                        both = x_ref[t, pol, pl.ds(cells_at, quarter), lanes].astype(f32)
                        cells = jnp.where(group == 0, both[:GROUP], both[GROUP:])
                        new.append(totals[c * pols + pol] + cells / mean)
                        codes.append((jnp.log(mean) * CODE_STEPS - 0.5).astype(i32))
                    out[t, :, lanes] = jnp.concatenate(codes, axis=0).astype(jnp.int16)
                return tuple(new)

            zero = jnp.zeros((GROUP, LANES), f32)
            totals = lax.fori_loop(
                0, dates, add_date, (zero,) * (pols * (cols // LANES)), unroll=2
            )
            for c, lanes in enumerate(tiles_of(cols)):
                total = jnp.concatenate(totals[c * pols : (c + 1) * pols], axis=0) * steps
                high = total.astype(i32)
                rest = ((total - high.astype(f32)) * REST_STEPS).astype(i32)
                out[dates, :, lanes] = high.astype(jnp.int16)
                out[dates + 1, :, lanes] = rest.astype(jnp.int16)


def copy_edges(x_ref, out, bottom, dates):
    pols = x_ref.shape[1]
    for t in range(0, dates, 2):
        for lanes in tiles_of(x_ref.shape[3]):
            images = []
            for n in range(2 * pols):
                image = x_ref[t + n // pols, n % pols, :, lanes].astype(f32)
                images.append(jnp.where(bottom == 1, image[16 - HALO :], image[:HALO]))
            line = t * pols * HALO
            out[line : line + 16, lanes] = jnp.concatenate(images, axis=0).astype(out.dtype)


def edges_kernel(x_ref, far_ref, near_ref, rows_ref, arrived):
    half = lax.axis_index("date") // 2
    dates, _, rows, _ = x_ref.shape
    sides = (half, 1 - half)
    copies = []
    for n, side in enumerate(sides):
        at = pl.multiple_of(side * (rows - 16), 16)
        copies.append(
            pltpu.make_async_copy(x_ref.at[:, :, pl.ds(at, 16)], rows_ref.at[n], arrived.at[n])
        )
        copies[n].start()
    for n, out_ref in enumerate((far_ref, near_ref)):
        copies[n].wait()
        copy_edges(rows_ref.at[n], out_ref, sides[n], dates)


def edge_rows(intensity):
    dates, pols, _, cols = intensity.shape
    return pl.pallas_call(
        edges_kernel,
        in_specs=[pl.BlockSpec(memory_space=pltpu.HBM)],
        out_specs=[whole()] * 2,
        out_shape=[pltpu.VMEM((dates * pols * HALO, cols), intensity.dtype)] * 2,
        scratch_shapes=[
            pltpu.VMEM((2, dates, pols, 16, cols), intensity.dtype),
            pltpu.SemaphoreType.DMA((2,)),
        ],
        compiler_params=params(),
        cost_estimate=SHORT,
        name="edge_rows",
    )(intensity)


def box_codes(intensity, halos, ks, parts, after=()):
    dates, pols, rows, cols = intensity.shape
    shape = (dates + 2, pols * GROUP, cols)
    if len(parts) > 1:
        shape = (len(parts),) + shape
    out_shape = [pltpu.VMEM(shape, jnp.int16)] * len(ks)
    scratch = [
        pltpu.VMEM((cols, cols), jnp.bfloat16),
        pltpu.VMEM((dates * pols, cols // LANES, rows // 2 + 32, LANES), f32),
    ]
    first_spec = whole()
    out_shape += [pltpu.VMEM((GROUP, LANES), f32)]
    if halos:
        scratch += [pltpu.VMEM((dates * pols * HALO, cols), f32)]
    else:
        first_spec = pl.BlockSpec(memory_space=pltpu.HBM)
        scratch += [pltpu.VMEM(intensity.shape, intensity.dtype), pltpu.SemaphoreType.DMA((4,))]
    return pl.pallas_call(
        functools.partial(box_kernel, ks, parts),
        in_specs=[first_spec] + [whole()] * len(halos) + [anywhere()] * len(after),
        out_specs=[whole()] * len(out_shape),
        out_shape=out_shape,
        scratch_shapes=scratch,
        compiler_params=params(),
        cost_estimate=SHORT,
        name="box_codes",
    )(intensity, *halos, *after)


def factor_kernel(table_ref, mask_ref, *refs):
    factor_ref = refs[-1]
    dates, lines, _ = mask_ref.shape

    width = 4

    def tiles(n, unused):
        ats = [pl.multiple_of((n * width + i) * GROUP, GROUP) for i in range(width)]

        def add_date(t, totals):
            flags = [mask_ref[t, pl.ds(at, GROUP)].astype(f32) for at in ats]
            new = [totals[0][i] + flags[i] for i in range(width)]
            weights = [table_ref[h, t] for h in range(HARMONICS)]
            return (new,) + tuple(
                [totals[h][i] + flags[i] * weights[h] for i in range(width)]
                for h in range(1, HARMONICS)
            )

        zero = jnp.zeros((GROUP, LANES), f32)
        totals = lax.fori_loop(0, dates, add_date, ([zero] * width,) * HARMONICS, unroll=8)
        for i, at in enumerate(ats):
            factor_tile(factor_ref, at, *[total[i] for total in totals])
        return unused

    lax.fori_loop(0, lines // (GROUP * width), tiles, 0)


def factor_tile(factor_ref, at, m0, c1, s1, c2, s2, c3, s3, c4, s4):
    normal = {
        (0, 0): 2.0 * m0 + NOISE,
        (1, 0): 2.0 * c1,
        (2, 0): 2.0 * s1,
        (3, 0): 2.0 * c2,
        (4, 0): 2.0 * s2,
        (1, 1): m0 + c2 + NOISE,
        (2, 1): s2,
        (3, 1): c1 + c3,
        (4, 1): s1 + s3,
        (2, 2): m0 - c2 + NOISE,
        (3, 2): s3 - s1,
        (4, 2): c1 - c3,
        (3, 3): m0 + c4 + NOISE,
        (4, 3): s4,
        (4, 4): m0 - c4 + NOISE,
        (5, 0): m0,
        (5, 1): c1,
        (5, 2): s1,
        (5, 3): c2,
        (5, 4): s2,
        (5, 5): m0 + NOISE,
    }
    lower = {}
    inverse = {}
    for i in range(STATES):
        for j in range(i + 1):
            total = normal[i, j]
            for k in range(j):
                total = total - lower[i, k] * lower[j, k]
            if i == j:
                inverse[i] = 1.0 / jnp.sqrt(total)
            else:
                lower[i, j] = total * inverse[j]
    planes = [lower[p] for p in PAIRS] + [inverse[i] for i in range(STATES)]
    for h, plane in enumerate(planes):
        factor_ref[h, pl.ds(at, GROUP)] = plane


def factor(table, lines, after=()):
    return pl.pallas_call(
        factor_kernel,
        in_specs=[scalars(), whole()] + [anywhere()] * len(after),
        out_specs=whole(),
        out_shape=jax.ShapeDtypeStruct((PLANES,) + lines.shape[1:], f32),
        compiler_params=params(),
        cost_estimate=SHORT,
        name="factor",
    )(table, lines, *after)


class Joined:
    def __init__(self, refs, start, length):
        self.lines = [(ref, n) for ref in refs for n in range(ref.shape[0])]
        self.lines = self.lines[start : start + length]
        self.shape = (length,)

    def __getitem__(self, index):
        ref, n = self.lines[index[0]]
        return ref[(n, *index[1:])]


def decode_ratio(block, dates, lanes):
    high = block[dates, :, lanes].astype(i32).astype(f32)
    rest = block[dates + 1, :, lanes].astype(i32).astype(f32)
    return high + rest * (1.0 / REST_STEPS)


def add_logs(block, table_ref, start, flag_of, sums, tiles):
    for t in range(block.shape[0] - 2):
        weights = [table_ref[n, start + t] for n in range(STATES - 1)]
        for c, lanes in enumerate(tiles):
            logs = block[t, :, lanes].astype(i32).astype(f32)
            flag = flag_of(t, c, lanes)
            vh = logs[GROUP:] * flag
            both = logs[:GROUP] * flag + vh
            sums[c][0] = sums[c][0] + both
            for n in range(1, STATES - 1):
                sums[c][n] = sums[c][n] + both * weights[n]
            sums[c][STATES - 1] = sums[c][STATES - 1] + vh


def right_of(sums, flag_sums, ratio, steps):
    logs = jnp.log(ratio * (1.0 / steps))
    both = logs[:GROUP] + logs[GROUP:]
    right = [total * (1.0 / CODE_STEPS) for total in sums]
    for n in range(STATES - 1):
        right[n] = right[n] + both * flag_sums[n]
    right[STATES - 1] = right[STATES - 1] + logs[GROUP:] * flag_sums[0]
    return right


def right_kernel(pieces, table_ref, *refs):
    flags_refs, near_ref = refs[:pieces], refs[pieces]
    other_refs = refs[pieces + 1 : pieces + 3]
    part_ref, ratio_ref, flags_out, lines = refs[-4:]
    d = lax.axis_index("date")
    r = lax.axis_index("row")
    dates, chunks, _ = flags_refs[0].shape
    parts, count, _, cols = near_ref.shape
    local = count - 2
    tiles = tiles_of(cols)
    zero = jnp.zeros((GROUP, LANES), f32)
    for k, flags_ref in enumerate(flags_refs):
        at = pl.multiple_of((r ^ k) * chunks, 16) if pieces > 1 else 0
        lines[:, pl.ds(at, chunks)] = flags_ref[...].astype(f32)
    for part in range(parts):
        start = (d // 2 if part else 1 - d // 2) * GROUP * len(tiles)
        sums = [[zero] * STATES for _ in tiles]
        flag_sums = [[zero] * (STATES - 1) for _ in tiles]
        blocks = [near_ref.at[part], Joined(other_refs, part * count, count)]
        for k in range(4):
            date = (d ^ k) * local

            def weigh(t, c, lanes):
                flag = lines[date + t, pl.ds(start + c, GROUP, stride=len(tiles))]
                if k >= 2:
                    flags_out[part, (k - 2) * local + t, :, lanes] = flag
                flag_sums[c][0] = flag_sums[c][0] + flag
                for n in range(1, STATES - 1):
                    flag_sums[c][n] = flag_sums[c][n] + flag * table_ref[n, date + t]
                return flag

            if k < 2:
                add_logs(blocks[k], table_ref, date, weigh, sums, tiles)
            else:
                for t in range(local):
                    for c, lanes in enumerate(tiles):
                        weigh(t, c, lanes)
        for c, lanes in enumerate(tiles):
            ratios = [decode_ratio(block, local, lanes) for block in blocks]
            ratio_ref[part, :, lanes] = ratios[0] + ratios[1]
            for n, total in enumerate(sums[c] + flag_sums[c]):
                part_ref[part, n, :, lanes] = total


def right_sides(table, flags, near):
    dates, chunks, _ = flags[0].shape
    parts, _, _, cols = near[0].shape
    local = near[0].shape[1] - 2
    shapes = [
        (parts, 2 * STATES - 1, GROUP, cols),
        (parts, 2 * GROUP, cols),
        (parts, 2 * local, GROUP, cols),
    ]
    return pl.pallas_call(
        functools.partial(right_kernel, len(flags)),
        in_specs=[scalars()] + [whole()] * (len(flags) + len(near)),
        out_specs=[whole()] * len(shapes),
        out_shape=[pltpu.VMEM(shape, f32) for shape in shapes],
        scratch_shapes=[pltpu.VMEM((dates, len(flags) * chunks, LANES), f32)],
        compiler_params=params(),
        cost_estimate=SHORT,
        name="right_sides",
    )(table, *flags, *near)


def finish_kernel(dates, table_ref, part_ref, ratio_ref, flags_ref, far_2, far_3, *refs):
    out_refs, right = refs[:-1], refs[-1]
    d = lax.axis_index("date")
    r = lax.axis_index("row")
    parts, _, _, cols = far_2.shape
    local = far_2.shape[1] - 2
    tiles = tiles_of(cols)
    for part in range(parts):
        sums = [[part_ref[part, n, :, lanes] for n in range(STATES)] for lanes in tiles]
        blocks = (far_2.at[part], far_3.at[part])
        for k, block in enumerate(blocks):

            def flag_of(t, c, lanes):
                return flags_ref[part, k * local + t, :, lanes]

            add_logs(block, table_ref, (d ^ (k + 2)) * local, flag_of, sums, tiles)
        start = (d // 2 if part else 1 - d // 2) * GROUP * len(tiles)
        for c, lanes in enumerate(tiles):
            ratio = ratio_ref[part, :, lanes]
            for block in blocks:
                ratio = ratio + decode_ratio(block, local, lanes)
            flag_sums = [part_ref[part, STATES + n, :, lanes] for n in range(STATES - 1)]
            rights = right_of(sums[c], flag_sums, ratio, ratio_steps(local) * dates)
            for n, total in enumerate(rights):
                right[n, pl.ds(start + c, GROUP, stride=len(tiles))] = total
    for k, out_ref in enumerate(out_refs):
        chunks = out_ref.shape[1]
        at = pl.multiple_of((r ^ k) * chunks, GROUP) if len(out_refs) > 1 else 0
        out_ref[...] = right[:, pl.ds(at, chunks)]


def finish_sides(table, parts, far, dates, pieces):
    cols = far[0].shape[3]
    lines = 2 * GROUP * cols // LANES
    return pl.pallas_call(
        functools.partial(finish_kernel, dates),
        in_specs=[scalars()] + [whole()] * (len(parts) + len(far)),
        out_specs=[whole()] * pieces,
        out_shape=[pltpu.VMEM((STATES, lines // pieces, LANES), f32)] * pieces,
        scratch_shapes=[pltpu.VMEM((STATES, lines, LANES), f32)],
        compiler_params=params(),
        cost_estimate=SHORT,
        name="finish_sides",
    )(table, *parts, *far)


def solve_kernel(factor_ref, *refs):
    out_ref = refs[-1]
    r = lax.axis_index("row")
    for n, right_ref in enumerate(refs[:-1]):
        chunks = right_ref.shape[1]
        start = (r ^ n) * chunks if len(refs) > 2 else 0
        for line in range(0, chunks, GROUP):
            at = pl.ds(pl.multiple_of(start + line, GROUP), GROUP)
            lower = {p: factor_ref[h, at] for h, p in enumerate(PAIRS)}
            inverse = [factor_ref[len(PAIRS) + h, at] for h in range(STATES)]
            middle = []
            for i in range(STATES):
                total = right_ref[i, line : line + GROUP]
                for k in range(i):
                    total = total - lower[i, k] * middle[k]
                middle.append(total * inverse[i])
            solved = [None] * STATES
            for i in reversed(range(STATES)):
                total = middle[i]
                for k in range(i + 1, STATES):
                    total = total - lower[k, i] * solved[k]
                solved[i] = total * inverse[i]
                out_ref[i, at] = solved[i]


def solve(factors, rights):
    return pl.pallas_call(
        solve_kernel,
        in_specs=[whole()] * (1 + len(rights)),
        out_specs=whole(),
        out_shape=jax.ShapeDtypeStruct((STATES,) + factors.shape[1:], f32),
        compiler_params=params(),
        cost_estimate=SHORT,
        name="solve",
    )(factors, *rights)


def harmonics(day_index):
    phase = day_index.astype(f32) * (2.0 * math.pi / 365.0)
    order = (np.arange(HARMONICS)[:, None] + 1) // 2
    sines = np.arange(HARMONICS)[:, None] % 2 == 0
    sines[0] = False
    angle = order.astype(np.float32) * phase[None, :]
    return jnp.where(sines, jnp.sin(angle), jnp.cos(angle))


def body(intensity, valid_mask, day_index):
    rows, cols = intensity.shape[2:]
    date_devices = lax.axis_size("date")
    row_devices = lax.axis_size("row")
    all_dates = valid_mask.shape[0]
    lines_count = rows * cols // date_devices // LANES
    chunks = lines_count // row_devices
    direct = row_devices in (2, 4) and chunks % 16 == 0

    def exchange(piece, axis, k):
        return lax.ppermute(piece, axis, partners(lax.axis_size(axis), k))

    lines = valid_mask.reshape(all_dates, lines_count, LANES)
    table = harmonics(day_index)
    half = date_devices // 2

    def halo(cells, upwards):
        pairs = []
        for d in range(date_devices):
            for r in range(row_devices - 1):
                pair = (d * row_devices + r, d * row_devices + r + 1)
                pairs.append(pair[::-1] if (d < half) == upwards else pair)
        return lax.ppermute(cells, ("date", "row"), pairs)

    in_hbm = pltpu.with_memory_space_constraint(intensity, pltpu.HBM)
    far_edge, near_edge = edge_rows(in_hbm)
    far_halo = halo(far_edge, True)
    near_halo = halo(near_edge, False)
    if direct:
        flags = cast_flags(lines, row_devices, after=(far_edge,))
        ready = flags[:1]
        flags = [flags[0]] + [exchange(flags[k], "row", k) for k in range(1, row_devices)]
    else:
        ready = ()
        flags = lax.all_to_all(
            valid_mask.astype(jnp.bfloat16), "row", split_axis=1, concat_axis=2, tiled=True
        )
        flags = [flags.reshape(all_dates, lines_count, LANES)]
    *far, done = box_codes(intensity, (far_halo,), (2, 3), (0, 1), after=(table, *ready))
    far = [exchange(far[0], "date", 2), exchange(far[1], "date", 3)]
    *near, done = box_codes(intensity, (near_halo,), (0, 1), (0, 1), after=(done,))
    other = near[1].reshape(-1, *near[1].shape[2:])
    count = other.shape[0]
    cut = 2 * count // 3
    other = [other[:cut], other[cut:]]
    other, flags = lax.optimization_barrier((other, flags))
    near = [near[0]] + [exchange(codes, "date", 1) for codes in other]
    factors = factor(table, lines, after=(done,))

    pieces = row_devices if direct else 1
    parts = right_sides(table, flags, near)
    rights = finish_sides(table, parts, far, all_dates, pieces)
    if direct:
        rights = [rights[0]] + [exchange(rights[k], "row", k) for k in range(1, row_devices)]
    else:
        rights = rights[0].reshape(STATES, 1, row_devices, chunks * LANES)
        rights = lax.all_to_all(rights, "row", split_axis=2, concat_axis=1, tiled=True)
        rights = [rights.reshape(STATES, lines_count, LANES)]
    return solve(factors, rights).reshape(STATES, row_devices, 1, chunks * LANES)


def solution(mesh):
    return jax.shard_map(
        body,
        mesh=mesh,
        in_specs=(
            P("date", None, ("tile", "row"), None),
            P(None, "tile", ("date", "row"), None),
            P(),
        ),
        out_specs=P(None, "tile", ("date", "row"), None),
        check_vma=False,
    )
```

```python
import functools
import math

import jax
import jax.numpy as jnp
import numpy as np
from jax import lax
from jax.experimental import pallas as pl
from jax.experimental.pallas import tpu as pltpu
from jax.sharding import PartitionSpec as P

RADIUS = 3
STATES = 6
HALO = 4
GROUP = 8
LANES = 128
HARMONICS = 9
NOISE = 0.05
CODE_STEPS = 8192.0
VMEM_BYTES = 16 * 1024 * 1024

SHORT = pl.CostEstimate(flops=1000, bytes_accessed=1000, transcendentals=0)

f32 = jnp.float32
i32 = jnp.int32
PAIRS = [(i, j) for i in range(STATES) for j in range(i)]
PLANES = len(PAIRS) + STATES


def partners(count, k):
    return [(i, i ^ k) for i in range(count)]


def edge_count(positions, length):
    lower = jnp.maximum(positions - RADIUS, 0)
    upper = jnp.minimum(positions + RADIUS, length - 1)
    return (upper - lower + 1).astype(f32)


def whole():
    return pl.BlockSpec(memory_space=pltpu.VMEM)


def anywhere():
    return pl.BlockSpec(memory_space=pl.ANY)


def scalars():
    return pl.BlockSpec(memory_space=pltpu.SMEM)


def params():
    return pltpu.CompilerParams(vmem_limit_bytes=VMEM_BYTES)


def tiles_of(width):
    return [slice(c, c + LANES) for c in range(0, width, LANES)]


def flags_kernel(ks, mask_ref, *refs):
    r = lax.axis_index("row")
    for k, out_ref in zip(ks, refs[-len(ks) :]):
        chunks = out_ref.shape[1]
        at = pl.multiple_of((r ^ k) * chunks, 16)
        out_ref[...] = mask_ref[:, pl.ds(at, chunks)].astype(f32).astype(jnp.bfloat16)


def cast_flags(lines, pieces, ks, after=()):
    dates, count, lanes = lines.shape
    return pl.pallas_call(
        functools.partial(flags_kernel, ks),
        in_specs=[whole()] + [anywhere()] * len(after),
        out_specs=[whole()] * len(ks),
        out_shape=[pltpu.VMEM((dates, count // pieces, lanes), jnp.bfloat16)] * len(ks),
        compiler_params=params(),
        cost_estimate=SHORT,
        name="cast_flags",
    )(lines, *after)


def box_kernel(ks, x_ref, *refs):
    halo_ref, band = refs[:2]
    *outs, token, sums, edges, scale_ref = refs[-4 - len(ks) :]
    token[...] = jnp.zeros_like(token)
    batch = 4
    d = lax.axis_index("date")
    r = lax.axis_index("row")
    dates, pols, rows, cols = x_ref.shape
    quarter = rows // lax.axis_size("date")
    half = (d ^ ks[0]) // 2
    span = rows // 2 + 16
    first = pl.multiple_of(half * (rows // 2 - 16), 16)
    images = dates * pols

    edges[...] = jnp.dot(halo_ref[...], band[...], preferred_element_type=f32)
    place = jnp.where(half == 0, GROUP - HALO, GROUP + span)
    for i in range(images):
        for c, lanes in enumerate(tiles_of(cols)):
            sums[i, c, pl.ds(place, HALO)] = edges[i * HALO : (i + 1) * HALO, lanes]
    for t in range(0, dates, batch):
        x = x_ref[t : t + batch, :, pl.ds(first, span), :].reshape(batch * pols * span, cols)
        summed = jnp.dot(x, band[...], preferred_element_type=f32)
        for i in range(batch * pols):
            for c, lanes in enumerate(tiles_of(cols)):
                sums[t * pols + i, c, GROUP : GROUP + span] = summed[
                    i * span : (i + 1) * span, lanes
                ]

    height = rows * lax.axis_size("row")
    col = edge_count(lax.broadcasted_iota(i32, (quarter, cols), 1), cols)
    for n, k in enumerate(ks):
        q = d ^ k
        top = pl.multiple_of(quarter * q, 16)
        base = GROUP + top - first
        row = edge_count(r * rows + top + lax.broadcasted_iota(i32, (quarter, cols), 0), height)
        scale_ref[...] = 1.0 / (row * col)
        groups = range(quarter // GROUP)
        places = [jnp.where(half == 0, 1 - g, g) for g in groups]

        def add_date(t, totals):
            new = []
            for c, lanes in enumerate(tiles_of(cols)):
                cells = [
                    x_ref[t, pol, pl.ds(top, quarter), lanes].astype(f32) for pol in range(pols)
                ]
                for g in groups:
                    down = slice(g * GROUP, (g + 1) * GROUP)
                    codes = []
                    for pol in range(pols):
                        i = t * pols + pol
                        start = base + g * GROUP
                        window = sums[i, c, pl.ds(start - RADIUS, GROUP)]
                        for shift in range(1 - RADIUS, RADIUS + 1):
                            window = window + sums[i, c, pl.ds(start + shift, GROUP)]
                        mean = window * scale_ref[down, lanes]
                        inverse = pl.reciprocal(mean, approx=True)
                        inverse = inverse * (2.0 - mean * inverse)
                        new.append(totals[len(new)] + cells[pol][down] * inverse)
                        codes.append((jnp.log(mean) * CODE_STEPS - 0.5).astype(i32))
                    codes = jnp.concatenate(codes, axis=0).astype(jnp.int16)
                    outs[n][places[g], t, :, lanes] = codes
            return tuple(new)

        zero = jnp.zeros((GROUP, LANES), f32)
        totals = (zero,) * (pols * quarter // GROUP * (cols // LANES))
        totals = list(lax.fori_loop(0, dates, add_date, totals, unroll=4))
        for lanes in tiles_of(cols):
            for g in groups:
                total = jnp.concatenate([totals.pop(0) for _ in range(pols)], axis=0)
                logs = jnp.log(total * (1.0 / dates)) * CODE_STEPS
                code = (logs + 32768.5).astype(i32) - 32768
                outs[n][places[g], dates, :, lanes] = code.astype(jnp.int16)


def copy_edges(x_ref, out, bottom, dates):
    pols = x_ref.shape[1]
    for t in range(0, dates, 2):
        for lanes in tiles_of(x_ref.shape[3]):
            images = []
            for n in range(2 * pols):
                image = x_ref[t + n // pols, n % pols, :, lanes].astype(f32)
                images.append(jnp.where(bottom == 1, image[16 - HALO :], image[:HALO]))
            line = t * pols * HALO
            out[line : line + 16, lanes] = jnp.concatenate(images, axis=0).astype(out.dtype)


def edges_kernel(x_ref, far_ref, near_ref, band_ref, rows_ref, arrived):
    half = lax.axis_index("date") // 2
    dates, _, rows, _ = x_ref.shape
    sides = (half, 1 - half)
    copies = []
    for n, side in enumerate(sides):
        at = pl.multiple_of(side * (rows - 16), 16)
        copies.append(
            pltpu.make_async_copy(x_ref.at[:, :, pl.ds(at, 16)], rows_ref.at[n], arrived.at[n])
        )
        copies[n].start()
    cols = x_ref.shape[3]
    near = (
        jnp.abs(
            lax.broadcasted_iota(i32, (cols, cols), 0) - lax.broadcasted_iota(i32, (cols, cols), 1)
        )
        <= RADIUS
    )
    band_ref[...] = near.astype(f32).astype(jnp.bfloat16)
    for n, out_ref in enumerate((far_ref, near_ref)):
        copies[n].wait()
        copy_edges(rows_ref.at[n], out_ref, sides[n], dates)


def edge_rows(intensity):
    dates, pols, _, cols = intensity.shape
    return pl.pallas_call(
        edges_kernel,
        in_specs=[pl.BlockSpec(memory_space=pltpu.HBM)],
        out_specs=[whole()] * 3,
        out_shape=[pltpu.VMEM((dates * pols * HALO, cols), intensity.dtype)] * 2
        + [pltpu.VMEM((cols, cols), jnp.bfloat16)],
        scratch_shapes=[
            pltpu.VMEM((2, dates, pols, 16, cols), intensity.dtype),
            pltpu.SemaphoreType.DMA((2,)),
        ],
        compiler_params=params(),
        cost_estimate=SHORT,
        name="edge_rows",
    )(intensity)


def box_codes(intensity, halo, band, ks, after=()):
    dates, pols, rows, cols = intensity.shape
    codes = pltpu.VMEM((2, dates + 1, pols * GROUP, cols), jnp.int16)
    out_shape = [codes] * len(ks) + [pltpu.VMEM((GROUP, LANES), f32)]
    return pl.pallas_call(
        functools.partial(box_kernel, ks),
        in_specs=[whole()] * 3 + [anywhere()] * len(after),
        out_specs=[whole()] * len(out_shape),
        out_shape=out_shape,
        scratch_shapes=[
            pltpu.VMEM((dates * pols, cols // LANES, rows // 2 + 32, LANES), f32),
            pltpu.VMEM((dates * pols * HALO, cols), f32),
            pltpu.VMEM((2 * GROUP, cols), f32),
        ],
        compiler_params=params(),
        cost_estimate=SHORT,
        name="box_codes",
    )(intensity, halo, band, *after)


def factor_kernel(table_ref, mask_ref, *refs):
    factor_ref = refs[-1]
    dates, lines, _ = mask_ref.shape

    width = 4

    def tiles(n, unused):
        ats = [pl.multiple_of((n * width + i) * GROUP, GROUP) for i in range(width)]

        def add_date(t, totals):
            flags = [mask_ref[t, pl.ds(at, GROUP)].astype(f32) for at in ats]
            new = [totals[0][i] + flags[i] for i in range(width)]
            weights = [table_ref[h, t] for h in range(HARMONICS)]
            return (new,) + tuple(
                [totals[h][i] + flags[i] * weights[h] for i in range(width)]
                for h in range(1, HARMONICS)
            )

        zero = jnp.zeros((GROUP, LANES), f32)
        totals = lax.fori_loop(0, dates, add_date, ([zero] * width,) * HARMONICS, unroll=8)
        for i, at in enumerate(ats):
            factor_tile(factor_ref, at, *[total[i] for total in totals])
        return unused

    lax.fori_loop(0, lines // (GROUP * width), tiles, 0)


def factor_tile(factor_ref, at, m0, c1, s1, c2, s2, c3, s3, c4, s4):
    normal = {
        (0, 0): 2.0 * m0 + NOISE,
        (1, 0): 2.0 * c1,
        (2, 0): 2.0 * s1,
        (3, 0): 2.0 * c2,
        (4, 0): 2.0 * s2,
        (1, 1): m0 + c2 + NOISE,
        (2, 1): s2,
        (3, 1): c1 + c3,
        (4, 1): s1 + s3,
        (2, 2): m0 - c2 + NOISE,
        (3, 2): s3 - s1,
        (4, 2): c1 - c3,
        (3, 3): m0 + c4 + NOISE,
        (4, 3): s4,
        (4, 4): m0 - c4 + NOISE,
        (5, 0): m0,
        (5, 1): c1,
        (5, 2): s1,
        (5, 3): c2,
        (5, 4): s2,
        (5, 5): m0 + NOISE,
    }
    lower = {}
    inverse = {}
    for i in range(STATES):
        for j in range(i + 1):
            total = normal[i, j]
            for k in range(j):
                total = total - lower[i, k] * lower[j, k]
            if i == j:
                inverse[i] = 1.0 / jnp.sqrt(total)
            else:
                lower[i, j] = total * inverse[j]
    planes = [lower[p] for p in PAIRS] + [inverse[i] for i in range(STATES)]
    for h, plane in enumerate(planes):
        factor_ref[h, pl.ds(at, GROUP)] = plane


def factor(table, lines, after=()):
    return pl.pallas_call(
        factor_kernel,
        in_specs=[scalars(), whole()] + [anywhere()] * len(after),
        out_specs=whole(),
        out_shape=jax.ShapeDtypeStruct((PLANES,) + lines.shape[1:], f32),
        compiler_params=params(),
        cost_estimate=SHORT,
        name="factor",
    )(table, lines, *after)


class Joined:
    def __init__(self, refs, start, length):
        self.lines = [(ref, n) for ref in refs for n in range(ref.shape[0])]
        self.lines = self.lines[start : start + length]
        self.shape = (length,)

    def __getitem__(self, index):
        ref, n = self.lines[index[0]]
        return ref[(n, *index[1:])]


def ratio_of(block, lanes):
    code = block[block.shape[0] - 1, :, lanes].astype(i32).astype(f32)
    return jnp.exp(code * (1.0 / CODE_STEPS))


def add_logs(block, table_ref, start, flag_of, sums, tiles):
    for t in range(block.shape[0] - 1):
        weights = [table_ref[n, start + t] for n in range(STATES - 1)]
        for c, lanes in enumerate(tiles):
            logs = block[t, :, lanes].astype(i32).astype(f32)
            flag = flag_of(t, c, lanes)
            vh = logs[GROUP:] * flag
            both = logs[:GROUP] * flag + vh
            sums[c][0] = sums[c][0] + both
            for n in range(1, STATES - 1):
                sums[c][n] = sums[c][n] + both * weights[n]
            sums[c][STATES - 1] = sums[c][STATES - 1] + vh


def right_of(sums, flag_sums, ratio, blocks):
    logs = jnp.log(ratio * (1.0 / blocks))
    both = logs[:GROUP] + logs[GROUP:]
    right = [total * (1.0 / CODE_STEPS) for total in sums]
    for n in range(STATES - 1):
        right[n] = right[n] + both * flag_sums[n]
    right[STATES - 1] = right[STATES - 1] + logs[GROUP:] * flag_sums[0]
    return right


def right_kernel(pieces, table_ref, *refs):
    flags_refs, near_ref = refs[:pieces], refs[pieces]
    other_refs = refs[pieces + 1 : pieces + 3]
    part_ref, ratio_ref, flags_out, lines = refs[-4:]
    d = lax.axis_index("date")
    r = lax.axis_index("row")
    dates, chunks, _ = flags_refs[0].shape
    parts, count, _, cols = near_ref.shape
    local = count - 1
    tiles = tiles_of(cols)
    zero = jnp.zeros((GROUP, LANES), f32)
    for k, flags_ref in enumerate(flags_refs):
        at = pl.multiple_of((r ^ k) * chunks, 16) if pieces > 1 else 0
        lines[:, pl.ds(at, chunks)] = flags_ref[...].astype(f32)
    for part in range(parts):
        start = (d // 2 if part else 1 - d // 2) * GROUP * len(tiles)
        sums = [[zero] * STATES for _ in tiles]
        flag_sums = [[zero] * (STATES - 1) for _ in tiles]
        blocks = [near_ref.at[part], Joined(other_refs, part * count, count)]
        for k in range(4):
            date = (d ^ k) * local

            def weigh(t, c, lanes):
                flag = lines[date + t, pl.ds(start + c, GROUP, stride=len(tiles))]
                if k >= 2:
                    flags_out[part, (k - 2) * local + t, :, lanes] = flag
                flag_sums[c][0] = flag_sums[c][0] + flag
                for n in range(1, STATES - 1):
                    flag_sums[c][n] = flag_sums[c][n] + flag * table_ref[n, date + t]
                return flag

            if k < 2:
                add_logs(blocks[k], table_ref, date, weigh, sums, tiles)
            else:
                for t in range(local):
                    for c, lanes in enumerate(tiles):
                        weigh(t, c, lanes)
        for c, lanes in enumerate(tiles):
            ratios = [ratio_of(block, lanes) for block in blocks]
            ratio_ref[part, :, lanes] = ratios[0] + ratios[1]
            for n, total in enumerate(sums[c] + flag_sums[c]):
                part_ref[part, n, :, lanes] = total


def right_sides(table, flags, near):
    dates, chunks, _ = flags[0].shape
    parts, _, _, cols = near[0].shape
    local = near[0].shape[1] - 1
    shapes = [
        (parts, 2 * STATES - 1, GROUP, cols),
        (parts, 2 * GROUP, cols),
        (parts, 2 * local, GROUP, cols),
    ]
    return pl.pallas_call(
        functools.partial(right_kernel, len(flags)),
        in_specs=[scalars()] + [whole()] * (len(flags) + len(near)),
        out_specs=[whole()] * len(shapes),
        out_shape=[pltpu.VMEM(shape, f32) for shape in shapes],
        scratch_shapes=[pltpu.VMEM((dates, len(flags) * chunks, LANES), f32)],
        compiler_params=params(),
        cost_estimate=SHORT,
        name="right_sides",
    )(table, *flags, *near)


def finish_kernel(dates, table_ref, part_ref, ratio_ref, flags_ref, far_2, far_3, *refs):
    out_refs, right = refs[:-1], refs[-1]
    d = lax.axis_index("date")
    r = lax.axis_index("row")
    parts, _, _, cols = far_2.shape
    local = far_2.shape[1] - 1
    tiles = tiles_of(cols)
    for part in range(parts):
        sums = [[part_ref[part, n, :, lanes] for n in range(STATES)] for lanes in tiles]
        blocks = (far_2.at[part], far_3.at[part])
        for k, block in enumerate(blocks):

            def flag_of(t, c, lanes):
                return flags_ref[part, k * local + t, :, lanes]

            add_logs(block, table_ref, (d ^ (k + 2)) * local, flag_of, sums, tiles)
        start = (d // 2 if part else 1 - d // 2) * GROUP * len(tiles)
        for c, lanes in enumerate(tiles):
            ratio = ratio_ref[part, :, lanes]
            for block in blocks:
                ratio = ratio + ratio_of(block, lanes)
            flag_sums = [part_ref[part, STATES + n, :, lanes] for n in range(STATES - 1)]
            rights = right_of(sums[c], flag_sums, ratio, dates // local)
            for n, total in enumerate(rights):
                right[n, pl.ds(start + c, GROUP, stride=len(tiles))] = total
    for k, out_ref in enumerate(out_refs):
        chunks = out_ref.shape[1]
        at = pl.multiple_of((r ^ k) * chunks, GROUP) if len(out_refs) > 1 else 0
        out_ref[...] = right[:, pl.ds(at, chunks)]


def finish_sides(table, parts, far, dates, pieces):
    cols = far[0].shape[3]
    lines = 2 * GROUP * cols // LANES
    return pl.pallas_call(
        functools.partial(finish_kernel, dates),
        in_specs=[scalars()] + [whole()] * (len(parts) + len(far)),
        out_specs=[whole()] * pieces,
        out_shape=[pltpu.VMEM((STATES, lines // pieces, LANES), f32)] * pieces,
        scratch_shapes=[pltpu.VMEM((STATES, lines, LANES), f32)],
        compiler_params=params(),
        cost_estimate=SHORT,
        name="finish_sides",
    )(table, *parts, *far)


def solve_kernel(factor_ref, *refs):
    out_ref = refs[-1]
    r = lax.axis_index("row")
    for n, right_ref in enumerate(refs[:-1]):
        chunks = right_ref.shape[1]
        start = (r ^ n) * chunks if len(refs) > 2 else 0
        for line in range(0, chunks, GROUP):
            at = pl.ds(pl.multiple_of(start + line, GROUP), GROUP)
            lower = {p: factor_ref[h, at] for h, p in enumerate(PAIRS)}
            inverse = [factor_ref[len(PAIRS) + h, at] for h in range(STATES)]
            middle = []
            for i in range(STATES):
                total = right_ref[i, line : line + GROUP]
                for k in range(i):
                    total = total - lower[i, k] * middle[k]
                middle.append(total * inverse[i])
            solved = [None] * STATES
            for i in reversed(range(STATES)):
                total = middle[i]
                for k in range(i + 1, STATES):
                    total = total - lower[k, i] * solved[k]
                solved[i] = total * inverse[i]
                out_ref[i, at] = solved[i]


def solve(factors, rights):
    return pl.pallas_call(
        solve_kernel,
        in_specs=[whole()] * (1 + len(rights)),
        out_specs=whole(),
        out_shape=jax.ShapeDtypeStruct((STATES,) + factors.shape[1:], f32),
        compiler_params=params(),
        cost_estimate=SHORT,
        name="solve",
    )(factors, *rights)


def harmonics(day_index):
    phase = day_index.astype(f32) * (2.0 * math.pi / 365.0)
    order = (np.arange(HARMONICS)[:, None] + 1) // 2
    sines = np.arange(HARMONICS)[:, None] % 2 == 0
    sines[0] = False
    angle = order.astype(np.float32) * phase[None, :]
    return jnp.where(sines, jnp.sin(angle), jnp.cos(angle))


def body(intensity, valid_mask, day_index):
    rows, cols = intensity.shape[2:]
    date_devices = lax.axis_size("date")
    row_devices = lax.axis_size("row")
    all_dates = valid_mask.shape[0]
    lines_count = rows * cols // date_devices // LANES
    chunks = lines_count // row_devices
    direct = row_devices in (2, 4) and chunks % 16 == 0

    def exchange(piece, axis, k):
        return lax.ppermute(piece, axis, partners(lax.axis_size(axis), k))

    lines = valid_mask.reshape(all_dates, lines_count, LANES)
    table = harmonics(day_index)
    half = date_devices // 2

    def halo(cells, upwards):
        pairs = []
        for d in range(date_devices):
            for r in range(row_devices - 1):
                pair = (d * row_devices + r, d * row_devices + r + 1)
                pairs.append(pair[::-1] if (d < half) == upwards else pair)
        return lax.ppermute(cells, ("date", "row"), pairs)

    in_hbm = pltpu.with_memory_space_constraint(intensity, pltpu.HBM)
    far_edge, near_edge, band = edge_rows(in_hbm)
    far_halo = halo(far_edge, True)
    near_halo = halo(near_edge, False)
    last = row_devices - 1
    ready = ()
    if direct:
        flags = dict(zip((0, last), cast_flags(lines, row_devices, (0, last), after=(far_edge,))))
        ready = (flags[0],)
        flags[last] = exchange(flags[last], "row", last)
    *far, done = box_codes(intensity, far_halo, band, (2, 3), after=(table, *ready))
    far = [exchange(far[0], "date", 2), exchange(far[1], "date", 3)]
    if direct:
        ks = tuple(range(1, last))
        for k, piece in zip(ks, cast_flags(lines, row_devices, ks, after=(done,)) if ks else ()):
            flags[k] = exchange(piece, "row", k)
        flags = [flags[k] for k in range(row_devices)]
        ready = (flags[last],)
    else:
        flags = lax.all_to_all(
            valid_mask.astype(jnp.bfloat16), "row", split_axis=1, concat_axis=2, tiled=True
        )
        flags = [flags.reshape(all_dates, lines_count, LANES)]
    *near, done = box_codes(intensity, near_halo, band, (0, 1), after=(done, *ready))
    near = [near[0], near[1]]
    factors = factor(table, lines, after=(done,))
    other = near[1].reshape(-1, *near[1].shape[2:])
    count = other.shape[0]
    cut = count // 2
    other = [other[:cut], other[cut:]]
    other, flags = lax.optimization_barrier((other, flags))
    near = [near[0]] + [exchange(codes, "date", 1) for codes in other]
    factors = factor(table, lines, after=(done,))

    pieces = row_devices if direct else 1
    parts = right_sides(table, flags, near)
    rights = finish_sides(table, parts, far, all_dates, pieces)
    if direct:
        rights = [rights[0]] + [exchange(rights[k], "row", k) for k in range(1, row_devices)]
    else:
        rights = rights[0].reshape(STATES, 1, row_devices, chunks * LANES)
        rights = lax.all_to_all(rights, "row", split_axis=2, concat_axis=1, tiled=True)
        rights = [rights.reshape(STATES, lines_count, LANES)]
    return solve(factors, rights).reshape(STATES, row_devices, 1, chunks * LANES)


def solution(mesh):
    return jax.shard_map(
        body,
        mesh=mesh,
        in_specs=(
            P("date", None, ("tile", "row"), None),
            P(None, "tile", ("date", "row"), None),
            P(),
        ),
        out_specs=P(None, "tile", ("date", "row"), None),
        check_vma=False,
    )
```

```python
import functools
import math

import jax
import jax.numpy as jnp
import numpy as np
from jax import lax
from jax.experimental import pallas as pl
from jax.experimental.pallas import tpu as pltpu
from jax.sharding import PartitionSpec as P

RADIUS = 3
STATES = 6
HALO = 4
GROUP = 8
LANES = 128
HARMONICS = 9
NOISE = 0.05
CODE_STEPS = 8192.0
VMEM_BYTES = 16 * 1024 * 1024

SHORT = pl.CostEstimate(flops=1000, bytes_accessed=1000, transcendentals=0)

f32 = jnp.float32
i32 = jnp.int32
PAIRS = [(i, j) for i in range(STATES) for j in range(i)]
PLANES = len(PAIRS) + STATES


def partners(count, k):
    return [(i, i ^ k) for i in range(count)]


def edge_count(positions, length):
    lower = jnp.maximum(positions - RADIUS, 0)
    upper = jnp.minimum(positions + RADIUS, length - 1)
    return (upper - lower + 1).astype(f32)


def whole():
    return pl.BlockSpec(memory_space=pltpu.VMEM)


def anywhere():
    return pl.BlockSpec(memory_space=pl.ANY)


def scalars():
    return pl.BlockSpec(memory_space=pltpu.SMEM)


def params():
    return pltpu.CompilerParams(vmem_limit_bytes=VMEM_BYTES)


def tiles_of(width):
    return [slice(c, c + LANES) for c in range(0, width, LANES)]


def flags_kernel(ks, mask_ref, *refs):
    r = lax.axis_index("row")
    for k, out_ref in zip(ks, refs[-len(ks) :]):
        chunks = out_ref.shape[1]
        at = pl.multiple_of((r ^ k) * chunks, 16)
        out_ref[...] = mask_ref[:, pl.ds(at, chunks)].astype(f32).astype(jnp.bfloat16)


def cast_flags(lines, pieces, ks, after=()):
    dates, count, lanes = lines.shape
    return pl.pallas_call(
        functools.partial(flags_kernel, ks),
        in_specs=[whole()] + [anywhere()] * len(after),
        out_specs=[whole()] * len(ks),
        out_shape=[pltpu.VMEM((dates, count // pieces, lanes), jnp.bfloat16)] * len(ks),
        compiler_params=params(),
        cost_estimate=SHORT,
        name="cast_flags",
    )(lines, *after)


def box_kernel(ks, x_ref, *refs):
    halo_ref, band = refs[:2]
    *outs, token, sums, edges, scale_ref = refs[-4 - len(ks) :]
    token[...] = jnp.zeros_like(token)
    batch = 4
    d = lax.axis_index("date")
    r = lax.axis_index("row")
    dates, pols, rows, cols = x_ref.shape
    quarter = rows // lax.axis_size("date")
    half = (d ^ ks[0]) // 2
    span = rows // 2 + 16
    first = pl.multiple_of(half * (rows // 2 - 16), 16)
    images = dates * pols

    edges[...] = jnp.dot(halo_ref[...], band[...], preferred_element_type=f32)
    place = jnp.where(half == 0, GROUP - HALO, GROUP + span)
    for i in range(images):
        for c, lanes in enumerate(tiles_of(cols)):
            sums[i, c, pl.ds(place, HALO)] = edges[i * HALO : (i + 1) * HALO, lanes]
    for t in range(0, dates, batch):
        x = x_ref[t : t + batch, :, pl.ds(first, span), :].reshape(batch * pols * span, cols)
        summed = jnp.dot(x, band[...], preferred_element_type=f32)
        for i in range(batch * pols):
            for c, lanes in enumerate(tiles_of(cols)):
                sums[t * pols + i, c, GROUP : GROUP + span] = summed[
                    i * span : (i + 1) * span, lanes
                ]

    height = rows * lax.axis_size("row")
    col = edge_count(lax.broadcasted_iota(i32, (quarter, cols), 1), cols)
    for n, k in enumerate(ks):
        q = d ^ k
        top = pl.multiple_of(quarter * q, 16)
        base = GROUP + top - first
        row = edge_count(r * rows + top + lax.broadcasted_iota(i32, (quarter, cols), 0), height)
        scale_ref[...] = 1.0 / (row * col)
        groups = range(quarter // GROUP)
        places = [jnp.where(half == 0, 1 - g, g) for g in groups]

        def add_date(t, totals):
            new = []
            for c, lanes in enumerate(tiles_of(cols)):
                cells = [
                    x_ref[t, pol, pl.ds(top, quarter), lanes].astype(f32) for pol in range(pols)
                ]
                for g in groups:
                    down = slice(g * GROUP, (g + 1) * GROUP)
                    codes = []
                    for pol in range(pols):
                        i = t * pols + pol
                        start = base + g * GROUP
                        window = sums[i, c, pl.ds(start - RADIUS, GROUP)]
                        for shift in range(1 - RADIUS, RADIUS + 1):
                            window = window + sums[i, c, pl.ds(start + shift, GROUP)]
                        mean = window * scale_ref[down, lanes]
                        inverse = pl.reciprocal(mean, approx=True)
                        inverse = inverse * (2.0 - mean * inverse)
                        new.append(totals[len(new)] + cells[pol][down] * inverse)
                        codes.append((jnp.log(mean) * CODE_STEPS - 0.5).astype(i32))
                    codes = jnp.concatenate(codes, axis=0).astype(jnp.int16)
                    outs[n][places[g], t, :, lanes] = codes
            return tuple(new)

        zero = jnp.zeros((GROUP, LANES), f32)
        totals = (zero,) * (pols * quarter // GROUP * (cols // LANES))
        totals = list(lax.fori_loop(0, dates, add_date, totals, unroll=4))
        for lanes in tiles_of(cols):
            for g in groups:
                total = jnp.concatenate([totals.pop(0) for _ in range(pols)], axis=0)
                logs = jnp.log(total * (1.0 / dates)) * CODE_STEPS
                code = (logs + 32768.5).astype(i32) - 32768
                outs[n][places[g], dates, :, lanes] = code.astype(jnp.int16)


def copy_edges(x_ref, out, bottom, dates):
    pols = x_ref.shape[1]
    for t in range(0, dates, 2):
        for lanes in tiles_of(x_ref.shape[3]):
            images = []
            for n in range(2 * pols):
                image = x_ref[t + n // pols, n % pols, :, lanes].astype(f32)
                images.append(jnp.where(bottom == 1, image[16 - HALO :], image[:HALO]))
            line = t * pols * HALO
            out[line : line + 16, lanes] = jnp.concatenate(images, axis=0).astype(out.dtype)


def edges_kernel(x_ref, far_ref, near_ref, band_ref, rows_ref, arrived):
    half = lax.axis_index("date") // 2
    dates, _, rows, _ = x_ref.shape
    sides = (half, 1 - half)
    copies = []
    for n, side in enumerate(sides):
        at = pl.multiple_of(side * (rows - 16), 16)
        copies.append(
            pltpu.make_async_copy(x_ref.at[:, :, pl.ds(at, 16)], rows_ref.at[n], arrived.at[n])
        )
        copies[n].start()
    cols = x_ref.shape[3]
    near = (
        jnp.abs(
            lax.broadcasted_iota(i32, (cols, cols), 0) - lax.broadcasted_iota(i32, (cols, cols), 1)
        )
        <= RADIUS
    )
    band_ref[...] = near.astype(f32).astype(jnp.bfloat16)
    for n, out_ref in enumerate((far_ref, near_ref)):
        copies[n].wait()
        copy_edges(rows_ref.at[n], out_ref, sides[n], dates)


def edge_rows(intensity):
    dates, pols, _, cols = intensity.shape
    return pl.pallas_call(
        edges_kernel,
        in_specs=[pl.BlockSpec(memory_space=pltpu.HBM)],
        out_specs=[whole()] * 3,
        out_shape=[pltpu.VMEM((dates * pols * HALO, cols), intensity.dtype)] * 2
        + [pltpu.VMEM((cols, cols), jnp.bfloat16)],
        scratch_shapes=[
            pltpu.VMEM((2, dates, pols, 16, cols), intensity.dtype),
            pltpu.SemaphoreType.DMA((2,)),
        ],
        compiler_params=params(),
        cost_estimate=SHORT,
        name="edge_rows",
    )(intensity)


def box_codes(intensity, halo, band, ks, after=()):
    dates, pols, rows, cols = intensity.shape
    codes = pltpu.VMEM((2, dates + 1, pols * GROUP, cols), jnp.int16)
    out_shape = [codes] * len(ks) + [pltpu.VMEM((GROUP, LANES), f32)]
    return pl.pallas_call(
        functools.partial(box_kernel, ks),
        in_specs=[whole()] * 3 + [anywhere()] * len(after),
        out_specs=[whole()] * len(out_shape),
        out_shape=out_shape,
        scratch_shapes=[
            pltpu.VMEM((dates * pols, cols // LANES, rows // 2 + 32, LANES), f32),
            pltpu.VMEM((dates * pols * HALO, cols), f32),
            pltpu.VMEM((2 * GROUP, cols), f32),
        ],
        compiler_params=params(),
        cost_estimate=SHORT,
        name="box_codes",
    )(intensity, halo, band, *after)


def factor_kernel(table_ref, mask_ref, *refs):
    factor_ref = refs[-1]
    dates, lines, _ = mask_ref.shape

    width = 4

    def tiles(n, unused):
        ats = [pl.multiple_of((n * width + i) * GROUP, GROUP) for i in range(width)]

        def add_date(t, totals):
            flags = [mask_ref[t, pl.ds(at, GROUP)].astype(f32) for at in ats]
            new = [totals[0][i] + flags[i] for i in range(width)]
            weights = [table_ref[h, t] for h in range(HARMONICS)]
            return (new,) + tuple(
                [totals[h][i] + flags[i] * weights[h] for i in range(width)]
                for h in range(1, HARMONICS)
            )

        zero = jnp.zeros((GROUP, LANES), f32)
        totals = lax.fori_loop(0, dates, add_date, ([zero] * width,) * HARMONICS, unroll=8)
        for i, at in enumerate(ats):
            factor_tile(factor_ref, at, *[total[i] for total in totals])
        return unused

    lax.fori_loop(0, lines // (GROUP * width), tiles, 0)


def factor_tile(factor_ref, at, m0, c1, s1, c2, s2, c3, s3, c4, s4):
    normal = {
        (0, 0): 2.0 * m0 + NOISE,
        (1, 0): 2.0 * c1,
        (2, 0): 2.0 * s1,
        (3, 0): 2.0 * c2,
        (4, 0): 2.0 * s2,
        (1, 1): m0 + c2 + NOISE,
        (2, 1): s2,
        (3, 1): c1 + c3,
        (4, 1): s1 + s3,
        (2, 2): m0 - c2 + NOISE,
        (3, 2): s3 - s1,
        (4, 2): c1 - c3,
        (3, 3): m0 + c4 + NOISE,
        (4, 3): s4,
        (4, 4): m0 - c4 + NOISE,
        (5, 0): m0,
        (5, 1): c1,
        (5, 2): s1,
        (5, 3): c2,
        (5, 4): s2,
        (5, 5): m0 + NOISE,
    }
    lower = {}
    inverse = {}
    for i in range(STATES):
        for j in range(i + 1):
            total = normal[i, j]
            for k in range(j):
                total = total - lower[i, k] * lower[j, k]
            if i == j:
                inverse[i] = 1.0 / jnp.sqrt(total)
            else:
                lower[i, j] = total * inverse[j]
    planes = [lower[p] for p in PAIRS] + [inverse[i] for i in range(STATES)]
    for h, plane in enumerate(planes):
        factor_ref[h, pl.ds(at, GROUP)] = plane


def factor(table, lines, after=()):
    return pl.pallas_call(
        factor_kernel,
        in_specs=[scalars(), whole()] + [anywhere()] * len(after),
        out_specs=whole(),
        out_shape=jax.ShapeDtypeStruct((PLANES,) + lines.shape[1:], f32),
        compiler_params=params(),
        cost_estimate=SHORT,
        name="factor",
    )(table, lines, *after)


class Joined:
    def __init__(self, refs, start, length):
        self.lines = [(ref, n) for ref in refs for n in range(ref.shape[0])]
        self.lines = self.lines[start : start + length]
        self.shape = (length,)

    def __getitem__(self, index):
        ref, n = self.lines[index[0]]
        return ref[(n, *index[1:])]


def ratio_of(block, lanes):
    code = block[block.shape[0] - 1, :, lanes].astype(i32).astype(f32)
    return jnp.exp(code * (1.0 / CODE_STEPS))


def add_logs(block, table_ref, start, flag_of, sums, tiles, more=None):
    for t in range(block.shape[0] - 1):
        weights = [table_ref[n, start + t] for n in range(STATES - 1)]
        for c, lanes in enumerate(tiles):
            logs = block[t, :, lanes].astype(i32).astype(f32)
            if more is not None:
                logs = logs + more[c]
            flag = flag_of(t, c, lanes)
            vh = logs[GROUP:] * flag
            both = logs[:GROUP] * flag + vh
            sums[c][0] = sums[c][0] + both
            for n in range(1, STATES - 1):
                sums[c][n] = sums[c][n] + both * weights[n]
            sums[c][STATES - 1] = sums[c][STATES - 1] + vh


def right_kernel(pieces, table_ref, *refs):
    flags_refs, near_ref = refs[:pieces], refs[pieces]
    other_refs = refs[pieces + 1 : pieces + 3]
    part_ref, ratio_ref, flags_out, lines = refs[-4:]
    d = lax.axis_index("date")
    r = lax.axis_index("row")
    dates, chunks, _ = flags_refs[0].shape
    parts, count, _, cols = near_ref.shape
    local = count - 1
    tiles = tiles_of(cols)
    zero = jnp.zeros((GROUP, LANES), f32)
    for k, flags_ref in enumerate(flags_refs):
        at = pl.multiple_of((r ^ k) * chunks, 16) if pieces > 1 else 0
        lines[:, pl.ds(at, chunks)] = flags_ref[...].astype(f32)
    for part in range(parts):
        start = (d // 2 if part else 1 - d // 2) * GROUP * len(tiles)
        sums = [[zero] * STATES for _ in tiles]
        flag_sums = [[zero] * (STATES - 1) for _ in tiles]
        blocks = [near_ref.at[part], Joined(other_refs, part * count, count)]
        for k in range(4):
            date = (d ^ k) * local

            def weigh(t, c, lanes):
                flag = lines[date + t, pl.ds(start + c, GROUP, stride=len(tiles))]
                flag_sums[c][0] = flag_sums[c][0] + flag
                for n in range(1, STATES - 1):
                    flag_sums[c][n] = flag_sums[c][n] + flag * table_ref[n, date + t]
                return flag

            if k < 2:
                add_logs(blocks[k], table_ref, date, weigh, sums, tiles)
            else:
                for t in range(local):
                    for c, lanes in enumerate(tiles):
                        flag = lines[date + t, pl.ds(start + c, GROUP, stride=len(tiles))]
                        flags_out[part, (k - 2) * local + t, :, lanes] = flag
        for c, lanes in enumerate(tiles):
            ratios = [ratio_of(block, lanes) for block in blocks]
            ratio_ref[part, :, lanes] = ratios[0] + ratios[1]
            for n, total in enumerate(sums[c] + flag_sums[c]):
                part_ref[part, n, :, lanes] = total


def right_sides(table, flags, near):
    dates, chunks, _ = flags[0].shape
    parts, _, _, cols = near[0].shape
    local = near[0].shape[1] - 1
    shapes = [
        (parts, 2 * STATES - 1, GROUP, cols),
        (parts, 2 * GROUP, cols),
        (parts, 2 * local, GROUP, cols),
    ]
    return pl.pallas_call(
        functools.partial(right_kernel, len(flags)),
        in_specs=[scalars()] + [whole()] * (len(flags) + len(near)),
        out_specs=[whole()] * len(shapes),
        out_shape=[pltpu.VMEM(shape, f32) for shape in shapes],
        scratch_shapes=[pltpu.VMEM((dates, len(flags) * chunks, LANES), f32)],
        compiler_params=params(),
        cost_estimate=SHORT,
        name="right_sides",
    )(table, *flags, *near)


def finish_kernel(dates, table_ref, part_ref, ratio_ref, flags_ref, far_2, far_3, *refs):
    out_refs, right = refs[:-1], refs[-1]
    d = lax.axis_index("date")
    r = lax.axis_index("row")
    parts, _, _, cols = far_2.shape
    local = far_2.shape[1] - 1
    tiles = tiles_of(cols)
    for part in range(parts):
        sums = [[part_ref[part, n, :, lanes] for n in range(STATES)] for lanes in tiles]
        blocks = (far_2.at[part], far_3.at[part])
        more = []
        for lanes in tiles:
            ratio = ratio_ref[part, :, lanes]
            for block in blocks:
                ratio = ratio + ratio_of(block, lanes)
            more.append(jnp.log(ratio * (local / dates)) * CODE_STEPS)
        for k, block in enumerate(blocks):

            def flag_of(t, c, lanes):
                return flags_ref[part, k * local + t, :, lanes]

            add_logs(block, table_ref, (d ^ (k + 2)) * local, flag_of, sums, tiles, more)
        start = (d // 2 if part else 1 - d // 2) * GROUP * len(tiles)
        for c, lanes in enumerate(tiles):
            flag_sums = [part_ref[part, STATES + n, :, lanes] for n in range(STATES - 1)]
            more_vh = more[c][GROUP:]
            both = more[c][:GROUP] + more_vh
            rights = [sums[c][n] + both * flag_sums[n] for n in range(STATES - 1)]
            rights.append(sums[c][STATES - 1] + more_vh * flag_sums[0])
            rights = [total * (1.0 / CODE_STEPS) for total in rights]
            for n, total in enumerate(rights):
                right[n, pl.ds(start + c, GROUP, stride=len(tiles))] = total
    for k, out_ref in enumerate(out_refs):
        chunks = out_ref.shape[1]
        at = pl.multiple_of((r ^ k) * chunks, GROUP) if len(out_refs) > 1 else 0
        out_ref[...] = right[:, pl.ds(at, chunks)]


def finish_sides(table, parts, far, dates, pieces):
    cols = far[0].shape[3]
    lines = 2 * GROUP * cols // LANES
    return pl.pallas_call(
        functools.partial(finish_kernel, dates),
        in_specs=[scalars()] + [whole()] * (len(parts) + len(far)),
        out_specs=[whole()] * pieces,
        out_shape=[pltpu.VMEM((STATES, lines // pieces, LANES), f32)] * pieces,
        scratch_shapes=[pltpu.VMEM((STATES, lines, LANES), f32)],
        compiler_params=params(),
        cost_estimate=SHORT,
        name="finish_sides",
    )(table, *parts, *far)


def solve_kernel(factor_ref, *refs):
    out_ref = refs[-1]
    r = lax.axis_index("row")
    for n, right_ref in enumerate(refs[:-1]):
        chunks = right_ref.shape[1]
        start = (r ^ n) * chunks if len(refs) > 2 else 0
        for line in range(0, chunks, GROUP):
            at = pl.ds(pl.multiple_of(start + line, GROUP), GROUP)
            lower = {p: factor_ref[h, at] for h, p in enumerate(PAIRS)}
            inverse = [factor_ref[len(PAIRS) + h, at] for h in range(STATES)]
            middle = []
            for i in range(STATES):
                total = right_ref[i, line : line + GROUP]
                for k in range(i):
                    total = total - lower[i, k] * middle[k]
                middle.append(total * inverse[i])
            solved = [None] * STATES
            for i in reversed(range(STATES)):
                total = middle[i]
                for k in range(i + 1, STATES):
                    total = total - lower[k, i] * solved[k]
                solved[i] = total * inverse[i]
                out_ref[i, at] = solved[i]


def solve(factors, rights):
    return pl.pallas_call(
        solve_kernel,
        in_specs=[whole()] * (1 + len(rights)),
        out_specs=whole(),
        out_shape=jax.ShapeDtypeStruct((STATES,) + factors.shape[1:], f32),
        compiler_params=params(),
        cost_estimate=SHORT,
        name="solve",
    )(factors, *rights)


def harmonics(day_index):
    phase = day_index.astype(f32) * (2.0 * math.pi / 365.0)
    order = (np.arange(HARMONICS)[:, None] + 1) // 2
    sines = np.arange(HARMONICS)[:, None] % 2 == 0
    sines[0] = False
    angle = order.astype(np.float32) * phase[None, :]
    return jnp.where(sines, jnp.sin(angle), jnp.cos(angle))


def body(intensity, valid_mask, day_index):
    rows, cols = intensity.shape[2:]
    date_devices = lax.axis_size("date")
    row_devices = lax.axis_size("row")
    all_dates = valid_mask.shape[0]
    lines_count = rows * cols // date_devices // LANES
    chunks = lines_count // row_devices
    direct = row_devices in (2, 4) and chunks % 16 == 0

    def exchange(piece, axis, k):
        return lax.ppermute(piece, axis, partners(lax.axis_size(axis), k))

    lines = valid_mask.reshape(all_dates, lines_count, LANES)
    table = harmonics(day_index)
    half = date_devices // 2

    def halo(cells, upwards):
        pairs = []
        for d in range(date_devices):
            for r in range(row_devices - 1):
                pair = (d * row_devices + r, d * row_devices + r + 1)
                pairs.append(pair[::-1] if (d < half) == upwards else pair)
        return lax.ppermute(cells, ("date", "row"), pairs)

    in_hbm = pltpu.with_memory_space_constraint(intensity, pltpu.HBM)
    far_edge, near_edge, band = edge_rows(in_hbm)
    far_halo = halo(far_edge, True)
    near_halo = halo(near_edge, False)
    last = row_devices - 1
    ready = ()
    if direct:
        flags = dict(zip((0, last), cast_flags(lines, row_devices, (0, last), after=(far_edge,))))
        ready = (flags[0],)
        flags[last] = exchange(flags[last], "row", last)
    *far, done = box_codes(intensity, far_halo, band, (2, 3), after=(table, *ready))
    far = [exchange(far[0], "date", 2), exchange(far[1], "date", 3)]
    if direct:
        ks = tuple(range(1, last))
        for k, piece in zip(ks, cast_flags(lines, row_devices, ks, after=(done,)) if ks else ()):
            flags[k] = exchange(piece, "row", k)
        flags = [flags[k] for k in range(row_devices)]
        ready = (flags[last],)
    else:
        flags = lax.all_to_all(
            valid_mask.astype(jnp.bfloat16), "row", split_axis=1, concat_axis=2, tiled=True
        )
        flags = [flags.reshape(all_dates, lines_count, LANES)]
    *near, done = box_codes(intensity, near_halo, band, (0, 1), after=(done, *ready))
    near = [near[0], near[1]]
    factors = factor(table, lines, after=(done,))
    other = near[1].reshape(-1, *near[1].shape[2:])
    count = other.shape[0]
    cut = count // 2
    other = [other[:cut], other[cut:]]
    other, flags = lax.optimization_barrier((other, flags))
    near = [near[0]] + [exchange(codes, "date", 1) for codes in other]
    factors = factor(table, lines, after=(done,))

    pieces = row_devices if direct else 1
    parts = right_sides(table, flags, near)
    rights = finish_sides(table, parts, far, all_dates, pieces)
    if direct:
        rights = [rights[0]] + [exchange(rights[k], "row", k) for k in range(1, row_devices)]
    else:
        rights = rights[0].reshape(STATES, 1, row_devices, chunks * LANES)
        rights = lax.all_to_all(rights, "row", split_axis=2, concat_axis=1, tiled=True)
        rights = [rights.reshape(STATES, lines_count, LANES)]
    return solve(factors, rights).reshape(STATES, row_devices, 1, chunks * LANES)


def solution(mesh):
    return jax.shard_map(
        body,
        mesh=mesh,
        in_specs=(
            P("date", None, ("tile", "row"), None),
            P(None, "tile", ("date", "row"), None),
            P(),
        ),
        out_specs=P(None, "tile", ("date", "row"), None),
        check_vma=False,
    )
```

```python
import functools
import math

import jax
import jax.numpy as jnp
import numpy as np
from jax import lax
from jax.experimental import pallas as pl
from jax.experimental.pallas import tpu as pltpu
from jax.sharding import PartitionSpec as P

RADIUS = 3
STATES = 6
HALO = 3
GROUP = 8
LANES = 128
HARMONICS = 9
NOISE = 0.05
CODE_STEPS = 8192.0
VMEM_BYTES = 16 * 1024 * 1024

SHORT = pl.CostEstimate(flops=1000, bytes_accessed=1000, transcendentals=0)

f32 = jnp.float32
i32 = jnp.int32
PAIRS = [(i, j) for i in range(STATES) for j in range(i)]
PLANES = len(PAIRS) + STATES


def partners(count, k):
    return [(i, i ^ k) for i in range(count)]


def edge_count(positions, length):
    lower = jnp.maximum(positions - RADIUS, 0)
    upper = jnp.minimum(positions + RADIUS, length - 1)
    return (upper - lower + 1).astype(f32)


def whole():
    return pl.BlockSpec(memory_space=pltpu.VMEM)


def anywhere():
    return pl.BlockSpec(memory_space=pl.ANY)


def scalars():
    return pl.BlockSpec(memory_space=pltpu.SMEM)


def params():
    return pltpu.CompilerParams(vmem_limit_bytes=VMEM_BYTES)


def tiles_of(width):
    return [slice(c, c + LANES) for c in range(0, width, LANES)]


def flags_kernel(ks, mask_ref, *refs):
    r = lax.axis_index("row")
    for k, out_ref in zip(ks, refs[-len(ks) :]):
        chunks = out_ref.shape[1]
        at = pl.multiple_of((r ^ k) * chunks, 16)
        out_ref[...] = mask_ref[:, pl.ds(at, chunks)].astype(f32).astype(jnp.bfloat16)


def cast_flags(lines, pieces, ks, after=()):
    dates, count, lanes = lines.shape
    return pl.pallas_call(
        functools.partial(flags_kernel, ks),
        in_specs=[whole()] + [anywhere()] * len(after),
        out_specs=[whole()] * len(ks),
        out_shape=[pltpu.VMEM((dates, count // pieces, lanes), jnp.bfloat16)] * len(ks),
        compiler_params=params(),
        cost_estimate=SHORT,
        name="cast_flags",
    )(lines, *after)


def box_kernel(ks, x_ref, *refs):
    halo_ref, band = refs[:2]
    *outs, token, sums, edges, scale_ref = refs[-4 - len(ks) :]
    token[...] = jnp.zeros_like(token)
    batch = 4
    d = lax.axis_index("date")
    r = lax.axis_index("row")
    dates, pols, rows, cols = x_ref.shape
    quarter = rows // lax.axis_size("date")
    half = (d ^ ks[0]) // 2
    span = rows // 2 + 16
    first = pl.multiple_of(half * (rows // 2 - 16), 16)
    images = dates * pols

    edges[...] = jnp.dot(halo_ref[...], band[...], preferred_element_type=f32)
    place = jnp.where(half == 0, GROUP - HALO, GROUP + span)
    for i in range(images):
        for c, lanes in enumerate(tiles_of(cols)):
            sums[i, c, pl.ds(place, HALO)] = edges[i * HALO : (i + 1) * HALO, lanes]
    for t in range(0, dates, batch):
        x = x_ref[t : t + batch, :, pl.ds(first, span), :].reshape(batch * pols * span, cols)
        summed = jnp.dot(x, band[...], preferred_element_type=f32)
        for i in range(batch * pols):
            for c, lanes in enumerate(tiles_of(cols)):
                sums[t * pols + i, c, GROUP : GROUP + span] = summed[
                    i * span : (i + 1) * span, lanes
                ]

    height = rows * lax.axis_size("row")
    col = edge_count(lax.broadcasted_iota(i32, (quarter, cols), 1), cols)
    for n, k in enumerate(ks):
        q = d ^ k
        top = pl.multiple_of(quarter * q, 16)
        base = GROUP + top - first
        row = edge_count(r * rows + top + lax.broadcasted_iota(i32, (quarter, cols), 0), height)
        scale_ref[...] = 1.0 / (row * col)
        groups = range(quarter // GROUP)
        places = [jnp.where(half == 0, 1 - g, g) for g in groups]

        def add_date(t, totals):
            new = []
            for c, lanes in enumerate(tiles_of(cols)):
                cells = [
                    x_ref[t, pol, pl.ds(top, quarter), lanes].astype(f32) for pol in range(pols)
                ]
                for g in groups:
                    down = slice(g * GROUP, (g + 1) * GROUP)
                    codes = []
                    for pol in range(pols):
                        i = t * pols + pol
                        start = base + g * GROUP
                        window = sums[i, c, pl.ds(start - RADIUS, GROUP)]
                        for shift in range(1 - RADIUS, RADIUS + 1):
                            window = window + sums[i, c, pl.ds(start + shift, GROUP)]
                        mean = window * scale_ref[down, lanes]
                        inverse = pl.reciprocal(mean, approx=True)
                        inverse = inverse * (2.0 - mean * inverse)
                        new.append(totals[len(new)] + cells[pol][down] * inverse)
                        codes.append((jnp.log(mean) * CODE_STEPS - 0.5).astype(i32))
                    codes = jnp.concatenate(codes, axis=0).astype(jnp.int16)
                    outs[n][places[g], t, :, lanes] = codes
            return tuple(new)

        zero = jnp.zeros((GROUP, LANES), f32)
        totals = (zero,) * (pols * quarter // GROUP * (cols // LANES))
        totals = list(lax.fori_loop(0, dates, add_date, totals, unroll=4))
        for lanes in tiles_of(cols):
            for g in groups:
                total = jnp.concatenate([totals.pop(0) for _ in range(pols)], axis=0)
                logs = jnp.log(total * (1.0 / dates)) * CODE_STEPS
                code = (logs + 32768.5).astype(i32) - 32768
                outs[n][places[g], dates, :, lanes] = code.astype(jnp.int16)


def copy_edges(x_ref, out, bottom, dates):
    pols = x_ref.shape[1]
    step = 16 // pols
    for t in range(0, dates, step):
        for lanes in tiles_of(x_ref.shape[3]):
            images = []
            for n in range(step * pols):
                image = x_ref[t + n // pols, n % pols, :, lanes].astype(f32)
                images.append(jnp.where(bottom == 1, image[16 - HALO :], image[:HALO]))
            line = t * pols * HALO
            out[line : line + 16 * HALO, lanes] = jnp.concatenate(images, axis=0).astype(out.dtype)


def edges_kernel(x_ref, far_ref, near_ref, band_ref, rows_ref, arrived):
    half = lax.axis_index("date") // 2
    dates, _, rows, _ = x_ref.shape
    sides = (half, 1 - half)
    copies = []
    for n, side in enumerate(sides):
        at = pl.multiple_of(side * (rows - 16), 16)
        copies.append(
            pltpu.make_async_copy(x_ref.at[:, :, pl.ds(at, 16)], rows_ref.at[n], arrived.at[n])
        )
        copies[n].start()
    cols = x_ref.shape[3]
    near = (
        jnp.abs(
            lax.broadcasted_iota(i32, (cols, cols), 0) - lax.broadcasted_iota(i32, (cols, cols), 1)
        )
        <= RADIUS
    )
    band_ref[...] = near.astype(f32).astype(jnp.bfloat16)
    for n, out_ref in enumerate((far_ref, near_ref)):
        copies[n].wait()
        copy_edges(rows_ref.at[n], out_ref, sides[n], dates)


def edge_rows(intensity):
    dates, pols, _, cols = intensity.shape
    return pl.pallas_call(
        edges_kernel,
        in_specs=[pl.BlockSpec(memory_space=pltpu.HBM)],
        out_specs=[whole()] * 3,
        out_shape=[pltpu.VMEM((dates * pols * HALO, cols), intensity.dtype)] * 2
        + [pltpu.VMEM((cols, cols), jnp.bfloat16)],
        scratch_shapes=[
            pltpu.VMEM((2, dates, pols, 16, cols), intensity.dtype),
            pltpu.SemaphoreType.DMA((2,)),
        ],
        compiler_params=params(),
        cost_estimate=SHORT,
        name="edge_rows",
    )(intensity)


def box_codes(intensity, halo, band, ks, after=()):
    dates, pols, rows, cols = intensity.shape
    codes = pltpu.VMEM((2, dates + 1, pols * GROUP, cols), jnp.int16)
    out_shape = [codes] * len(ks) + [pltpu.VMEM((GROUP, LANES), f32)]
    return pl.pallas_call(
        functools.partial(box_kernel, ks),
        in_specs=[whole()] * 3 + [anywhere()] * len(after),
        out_specs=[whole()] * len(out_shape),
        out_shape=out_shape,
        scratch_shapes=[
            pltpu.VMEM((dates * pols, cols // LANES, rows // 2 + 32, LANES), f32),
            pltpu.VMEM((dates * pols * HALO, cols), f32),
            pltpu.VMEM((2 * GROUP, cols), f32),
        ],
        compiler_params=params(),
        cost_estimate=SHORT,
        name="box_codes",
    )(intensity, halo, band, *after)


def factor_kernel(table_ref, mask_ref, *refs):
    factor_ref = refs[-1]
    dates, lines, _ = mask_ref.shape

    width = 4

    def tiles(n, unused):
        ats = [pl.multiple_of((n * width + i) * GROUP, GROUP) for i in range(width)]

        def add_date(t, totals):
            flags = [mask_ref[t, pl.ds(at, GROUP)].astype(f32) for at in ats]
            new = [totals[0][i] + flags[i] for i in range(width)]
            weights = [table_ref[h, t] for h in range(HARMONICS)]
            return (new,) + tuple(
                [totals[h][i] + flags[i] * weights[h] for i in range(width)]
                for h in range(1, HARMONICS)
            )

        zero = jnp.zeros((GROUP, LANES), f32)
        totals = lax.fori_loop(0, dates, add_date, ([zero] * width,) * HARMONICS, unroll=8)
        for i, at in enumerate(ats):
            factor_tile(factor_ref, at, *[total[i] for total in totals])
        return unused

    lax.fori_loop(0, lines // (GROUP * width), tiles, 0)


def factor_tile(factor_ref, at, m0, c1, s1, c2, s2, c3, s3, c4, s4):
    normal = {
        (0, 0): 2.0 * m0 + NOISE,
        (1, 0): 2.0 * c1,
        (2, 0): 2.0 * s1,
        (3, 0): 2.0 * c2,
        (4, 0): 2.0 * s2,
        (1, 1): m0 + c2 + NOISE,
        (2, 1): s2,
        (3, 1): c1 + c3,
        (4, 1): s1 + s3,
        (2, 2): m0 - c2 + NOISE,
        (3, 2): s3 - s1,
        (4, 2): c1 - c3,
        (3, 3): m0 + c4 + NOISE,
        (4, 3): s4,
        (4, 4): m0 - c4 + NOISE,
        (5, 0): m0,
        (5, 1): c1,
        (5, 2): s1,
        (5, 3): c2,
        (5, 4): s2,
        (5, 5): m0 + NOISE,
    }
    lower = {}
    inverse = {}
    for i in range(STATES):
        for j in range(i + 1):
            total = normal[i, j]
            for k in range(j):
                total = total - lower[i, k] * lower[j, k]
            if i == j:
                inverse[i] = 1.0 / jnp.sqrt(total)
            else:
                lower[i, j] = total * inverse[j]
    planes = [lower[p] for p in PAIRS] + [inverse[i] for i in range(STATES)]
    for h, plane in enumerate(planes):
        factor_ref[h, pl.ds(at, GROUP)] = plane


def factor(table, lines, after=()):
    return pl.pallas_call(
        factor_kernel,
        in_specs=[scalars(), whole()] + [anywhere()] * len(after),
        out_specs=whole(),
        out_shape=jax.ShapeDtypeStruct((PLANES,) + lines.shape[1:], f32),
        compiler_params=params(),
        cost_estimate=SHORT,
        name="factor",
    )(table, lines, *after)


class Joined:
    def __init__(self, refs, start, length):
        self.lines = [(ref, n) for ref in refs for n in range(ref.shape[0])]
        self.lines = self.lines[start : start + length]
        self.shape = (length,)

    def __getitem__(self, index):
        ref, n = self.lines[index[0]]
        return ref[(n, *index[1:])]


def ratio_of(block, lanes):
    code = block[block.shape[0] - 1, :, lanes].astype(i32).astype(f32)
    return jnp.exp(code * (1.0 / CODE_STEPS))


def add_logs(block, table_ref, start, flag_of, sums, tiles, more=None):
    for t in range(block.shape[0] - 1):
        weights = [table_ref[n, start + t] for n in range(STATES - 1)]
        for c, lanes in enumerate(tiles):
            logs = block[t, :, lanes].astype(i32).astype(f32)
            if more is not None:
                logs = logs + more[c]
            flag = flag_of(t, c, lanes)
            vh = logs[GROUP:] * flag
            both = logs[:GROUP] * flag + vh
            sums[c][0] = sums[c][0] + both
            for n in range(1, STATES - 1):
                sums[c][n] = sums[c][n] + both * weights[n]
            sums[c][STATES - 1] = sums[c][STATES - 1] + vh


def right_kernel(pieces, table_ref, *refs):
    flags_refs, near_ref = refs[:pieces], refs[pieces]
    other_refs = refs[pieces + 1 : pieces + 3]
    part_ref, ratio_ref, flags_out, lines = refs[-4:]
    d = lax.axis_index("date")
    r = lax.axis_index("row")
    dates, chunks, _ = flags_refs[0].shape
    parts, count, _, cols = near_ref.shape
    local = count - 1
    tiles = tiles_of(cols)
    zero = jnp.zeros((GROUP, LANES), f32)
    for k, flags_ref in enumerate(flags_refs):
        at = pl.multiple_of((r ^ k) * chunks, 16) if pieces > 1 else 0
        lines[:, pl.ds(at, chunks)] = flags_ref[...].astype(f32)
    for part in range(parts):
        start = (d // 2 if part else 1 - d // 2) * GROUP * len(tiles)
        sums = [[zero] * STATES for _ in tiles]
        flag_sums = [[zero] * (STATES - 1) for _ in tiles]
        blocks = [near_ref.at[part], Joined(other_refs, part * count, count)]
        for k in range(4):
            date = (d ^ k) * local

            def weigh(t, c, lanes):
                flag = lines[date + t, pl.ds(start + c, GROUP, stride=len(tiles))]
                flag_sums[c][0] = flag_sums[c][0] + flag
                for n in range(1, STATES - 1):
                    flag_sums[c][n] = flag_sums[c][n] + flag * table_ref[n, date + t]
                return flag

            if k < 2:
                add_logs(blocks[k], table_ref, date, weigh, sums, tiles)
            else:
                for t in range(local):
                    for c, lanes in enumerate(tiles):
                        flag = lines[date + t, pl.ds(start + c, GROUP, stride=len(tiles))]
                        flags_out[part, (k - 2) * local + t, :, lanes] = flag
        for c, lanes in enumerate(tiles):
            ratios = [ratio_of(block, lanes) for block in blocks]
            ratio_ref[part, :, lanes] = ratios[0] + ratios[1]
            for n, total in enumerate(sums[c] + flag_sums[c]):
                part_ref[part, n, :, lanes] = total


def right_sides(table, flags, near):
    dates, chunks, _ = flags[0].shape
    parts, _, _, cols = near[0].shape
    local = near[0].shape[1] - 1
    shapes = [
        (parts, 2 * STATES - 1, GROUP, cols),
        (parts, 2 * GROUP, cols),
        (parts, 2 * local, GROUP, cols),
    ]
    return pl.pallas_call(
        functools.partial(right_kernel, len(flags)),
        in_specs=[scalars()] + [whole()] * (len(flags) + len(near)),
        out_specs=[whole()] * len(shapes),
        out_shape=[pltpu.VMEM(shape, f32) for shape in shapes],
        scratch_shapes=[pltpu.VMEM((dates, len(flags) * chunks, LANES), f32)],
        compiler_params=params(),
        cost_estimate=SHORT,
        name="right_sides",
    )(table, *flags, *near)


def finish_kernel(dates, table_ref, part_ref, ratio_ref, flags_ref, far_2, far_3, *refs):
    out_refs, right = refs[:-1], refs[-1]
    d = lax.axis_index("date")
    r = lax.axis_index("row")
    parts, _, _, cols = far_2.shape
    local = far_2.shape[1] - 1
    tiles = tiles_of(cols)
    for part in range(parts):
        sums = [[part_ref[part, n, :, lanes] for n in range(STATES)] for lanes in tiles]
        blocks = (far_2.at[part], far_3.at[part])
        more = []
        for lanes in tiles:
            ratio = ratio_ref[part, :, lanes]
            for block in blocks:
                ratio = ratio + ratio_of(block, lanes)
            more.append(jnp.log(ratio * (local / dates)) * CODE_STEPS)
        for k, block in enumerate(blocks):

            def flag_of(t, c, lanes):
                return flags_ref[part, k * local + t, :, lanes]

            add_logs(block, table_ref, (d ^ (k + 2)) * local, flag_of, sums, tiles, more)
        start = (d // 2 if part else 1 - d // 2) * GROUP * len(tiles)
        for c, lanes in enumerate(tiles):
            flag_sums = [part_ref[part, STATES + n, :, lanes] for n in range(STATES - 1)]
            more_vh = more[c][GROUP:]
            both = more[c][:GROUP] + more_vh
            rights = [sums[c][n] + both * flag_sums[n] for n in range(STATES - 1)]
            rights.append(sums[c][STATES - 1] + more_vh * flag_sums[0])
            rights = [total * (1.0 / CODE_STEPS) for total in rights]
            for n, total in enumerate(rights):
                right[n, pl.ds(start + c, GROUP, stride=len(tiles))] = total
    for k, out_ref in enumerate(out_refs):
        chunks = out_ref.shape[1]
        at = pl.multiple_of((r ^ k) * chunks, GROUP) if len(out_refs) > 1 else 0
        out_ref[...] = right[:, pl.ds(at, chunks)]


def finish_sides(table, parts, far, dates, pieces):
    cols = far[0].shape[3]
    lines = 2 * GROUP * cols // LANES
    return pl.pallas_call(
        functools.partial(finish_kernel, dates),
        in_specs=[scalars()] + [whole()] * (len(parts) + len(far)),
        out_specs=[whole()] * pieces,
        out_shape=[pltpu.VMEM((STATES, lines // pieces, LANES), f32)] * pieces,
        scratch_shapes=[pltpu.VMEM((STATES, lines, LANES), f32)],
        compiler_params=params(),
        cost_estimate=SHORT,
        name="finish_sides",
    )(table, *parts, *far)


def solve_kernel(factor_ref, *refs):
    out_ref = refs[-1]
    r = lax.axis_index("row")
    for n, right_ref in enumerate(refs[:-1]):
        chunks = right_ref.shape[1]
        start = (r ^ n) * chunks if len(refs) > 2 else 0
        for line in range(0, chunks, GROUP):
            at = pl.ds(pl.multiple_of(start + line, GROUP), GROUP)
            lower = {p: factor_ref[h, at] for h, p in enumerate(PAIRS)}
            inverse = [factor_ref[len(PAIRS) + h, at] for h in range(STATES)]
            middle = []
            for i in range(STATES):
                total = right_ref[i, line : line + GROUP]
                for k in range(i):
                    total = total - lower[i, k] * middle[k]
                middle.append(total * inverse[i])
            solved = [None] * STATES
            for i in reversed(range(STATES)):
                total = middle[i]
                for k in range(i + 1, STATES):
                    total = total - lower[k, i] * solved[k]
                solved[i] = total * inverse[i]
                out_ref[i, at] = solved[i]


def solve(factors, rights):
    return pl.pallas_call(
        solve_kernel,
        in_specs=[whole()] * (1 + len(rights)),
        out_specs=whole(),
        out_shape=jax.ShapeDtypeStruct((STATES,) + factors.shape[1:], f32),
        compiler_params=params(),
        cost_estimate=SHORT,
        name="solve",
    )(factors, *rights)


def harmonics(day_index):
    phase = day_index.astype(f32) * (2.0 * math.pi / 365.0)
    order = (np.arange(HARMONICS)[:, None] + 1) // 2
    sines = np.arange(HARMONICS)[:, None] % 2 == 0
    sines[0] = False
    angle = order.astype(np.float32) * phase[None, :]
    return jnp.where(sines, jnp.sin(angle), jnp.cos(angle))


def body(intensity, valid_mask, day_index):
    rows, cols = intensity.shape[2:]
    date_devices = lax.axis_size("date")
    row_devices = lax.axis_size("row")
    all_dates = valid_mask.shape[0]
    lines_count = rows * cols // date_devices // LANES
    chunks = lines_count // row_devices
    direct = row_devices in (2, 4) and chunks % 16 == 0

    def exchange(piece, axis, k):
        return lax.ppermute(piece, axis, partners(lax.axis_size(axis), k))

    lines = valid_mask.reshape(all_dates, lines_count, LANES)
    table = harmonics(day_index)
    half = date_devices // 2

    def halo(cells, upwards):
        pairs = []
        for d in range(date_devices):
            for r in range(row_devices - 1):
                pair = (d * row_devices + r, d * row_devices + r + 1)
                pairs.append(pair[::-1] if (d < half) == upwards else pair)
        return lax.ppermute(cells, ("date", "row"), pairs)

    in_hbm = pltpu.with_memory_space_constraint(intensity, pltpu.HBM)
    far_edge, near_edge, band = edge_rows(in_hbm)
    far_halo = halo(far_edge, True)
    near_halo = halo(near_edge, False)
    last = row_devices - 1
    ready = ()
    if direct:
        flags = dict(zip((0, last), cast_flags(lines, row_devices, (0, last), after=(far_edge,))))
        ready = (flags[0],)
        flags[last] = exchange(flags[last], "row", last)
    *far, done = box_codes(intensity, far_halo, band, (2, 3), after=(table, *ready))
    far = [exchange(far[0], "date", 2), exchange(far[1], "date", 3)]
    if direct:
        ks = tuple(range(1, last))
        for k, piece in zip(ks, cast_flags(lines, row_devices, ks, after=(done,)) if ks else ()):
            flags[k] = exchange(piece, "row", k)
        flags = [flags[k] for k in range(row_devices)]
        ready = (flags[last],)
    else:
        flags = lax.all_to_all(
            valid_mask.astype(jnp.bfloat16), "row", split_axis=1, concat_axis=2, tiled=True
        )
        flags = [flags.reshape(all_dates, lines_count, LANES)]
    *near, done = box_codes(intensity, near_halo, band, (0, 1), after=(done, *ready))
    near = [near[0], near[1]]
    factors = factor(table, lines, after=(done,))
    other = near[1].reshape(-1, *near[1].shape[2:])
    count = other.shape[0]
    cut = count // 2
    other = [other[:cut], other[cut:]]
    other, flags = lax.optimization_barrier((other, flags))
    near = [near[0]] + [exchange(codes, "date", 1) for codes in other]
    factors = factor(table, lines, after=(done,))

    pieces = row_devices if direct else 1
    parts = right_sides(table, flags, near)
    rights = finish_sides(table, parts, far, all_dates, pieces)
    if direct:
        rights = [rights[0]] + [exchange(rights[k], "row", k) for k in range(1, row_devices)]
    else:
        rights = rights[0].reshape(STATES, 1, row_devices, chunks * LANES)
        rights = lax.all_to_all(rights, "row", split_axis=2, concat_axis=1, tiled=True)
        rights = [rights.reshape(STATES, lines_count, LANES)]
    return solve(factors, rights).reshape(STATES, row_devices, 1, chunks * LANES)


def solution(mesh):
    return jax.shard_map(
        body,
        mesh=mesh,
        in_specs=(
            P("date", None, ("tile", "row"), None),
            P(None, "tile", ("date", "row"), None),
            P(),
        ),
        out_specs=P(None, "tile", ("date", "row"), None),
        check_vma=False,
    )
```
